512 devices in a mesh: dp: 64 (over z_lo, y, core), feat: 8 (over z_hi, x).
Axes of the slice: x: 4, y: 4, z: 16 (z_hi: 2, z_lo: 8; z = z_hi * 8 + z_lo), core: 2. Of those that a mesh axis runs over, the one named last changes fastest.
Arguments:
- view_a: bfloat16 [512, 16384], P('dp', 'feat'), may hold values from -100 to 100
- view_b: bfloat16 [512, 16384], P('dp'), may hold values from -100 to 100
Outputs:
- correlation: float32 [16384, 16384], P('feat', 'dp')
- grad_a: float32 [512, 16384], P('dp', 'feat')
- grad_b: float32 [512, 16384], P(None, 'dp')
The draws below stay inside these ranges and needn't reach their ends.
All inputs are finite; a program needn't handle non-finite values.
Results may differ from the reference program's by a relative error of at most 0.0065.
Values may be sent and summed in bfloat16 or wider, within the bound.
No kernel may reach another device: no remote copies, remote signals or barrier semaphores. Data moves between devices by JAX's collectives and lax.ppermute only.
A program may use at most 64 MiB of HBM per device.

```python
import math
import jax
import jax.numpy as jnp
from jax import lax

WIDTH = 16384
IMAGES = 512
N_FEAT = 8


def mixed_noise(key):
    normal_part = jnp.clip(jax.random.normal(key, (IMAGES, WIDTH), jnp.float32), -4.0, 4.0)
    return normal_part


def build_view(key, shared):
    key_noise, key_cols, key_rows, key_mean = jax.random.split(key, 4)
    own_noise = mixed_noise(key_noise)
    col_scale = jnp.exp(jax.random.uniform(key_cols, (WIDTH,), jnp.float32, math.log(0.03), math.log(0.3)))
    ramp = 1.0 + 2.0 * jnp.arange(IMAGES, dtype=jnp.float32)[:, None] / (IMAGES - 1)
    row_scale = jnp.exp(jax.random.uniform(key_rows, (IMAGES, 1), jnp.float32, 0.0, math.log(10.0))) * ramp
    col_mean = jax.random.uniform(key_mean, (WIDTH,), jnp.float32, -1.0, 1.0)
    return col_mean + col_scale * row_scale * (shared + 0.6 * own_noise)


def draw_view_a(key, part):
    shared = mixed_noise(jax.random.fold_in(key, 101))
    key = jax.random.fold_in(key, 1)
    return build_view(key, shared).astype(jnp.bfloat16)


def draw_view_b(key, part):
    shared = mixed_noise(jax.random.fold_in(key, 101))
    key = jax.random.fold_in(key, 2)
    return build_view(key, shared).astype(jnp.bfloat16)


def setup_inputs(seed: int = 0) -> dict:
    key_of = jax.random.split(jax.random.key(seed), 3)
    return {
        "view_a": draw_view_a(jax.random.fold_in(key_of[2], 71), 0),
        "view_b": draw_view_b(jax.random.fold_in(key_of[2], 71), 0),
    }


epsilon = 1e-05
off_weight = 0.005

def standardize(values, images):
    as_float = values.astype(jnp.float32)
    column_mean = lax.optimization_barrier(jnp.sum(as_float, 0)) / images
    variance = lax.optimization_barrier(jnp.sum(as_float * as_float, 0)) / images - column_mean * column_mean
    inverse = lax.rsqrt(variance + epsilon)
    return (((as_float - column_mean) * inverse).astype(jnp.bfloat16), inverse)

def backward(grad_n, normed, inverse):
    as_float = normed.astype(jnp.float32)
    return (grad_n - as_float * lax.optimization_barrier(jnp.mean(grad_n * as_float, 0))) * inverse

def reference(view_a, view_b):
    images = view_a.shape[0]
    width = view_a.shape[1]
    norm_a, inverse_a = standardize(view_a, images)
    norm_b, inverse_b = standardize(view_b, images)
    float_b = norm_b.astype(jnp.float32)
    block_cols = width // N_FEAT
    blocks = norm_a.reshape(images, N_FEAT, block_cols).transpose(1, 0, 2)
    starts = jnp.arange(N_FEAT, dtype=jnp.int32) * block_cols

    def advance(carry_b, packed):
        a_block, first_row = packed
        correlation = lax.dot_general(a_block, norm_b, (((0,), (0,)), ((), ())), preferred_element_type=jnp.float32) / images
        row_ids = first_row + lax.iota(jnp.int32, block_cols)
        col_ids = lax.iota(jnp.int32, width)
        on_diag = row_ids[:, None] == col_ids[None, :]
        diagonal = lax.optimization_barrier(jnp.sum(jnp.where(on_diag, correlation, 0.0), 1))
        shift = -2.0 * (1.0 - diagonal) - 2.0 * off_weight * diagonal
        grad_tile = 2.0 * off_weight * correlation + jnp.where(on_diag, shift[:, None], 0.0)
        grad_a_n = lax.dot_general(float_b, grad_tile, (((1,), (1,)), ((), ())), precision=lax.Precision.HIGHEST, preferred_element_type=jnp.float32)
        carry_b = carry_b + jnp.dot(a_block.astype(jnp.float32), grad_tile, precision=lax.Precision.HIGHEST)
        return (carry_b, (correlation, grad_a_n))
    grad_b_n, (corr_blocks, grad_blocks) = lax.scan(advance, jnp.zeros((images, width), jnp.float32), (blocks, starts))
    correlation = corr_blocks.reshape(width, width)
    grad_a_n = grad_blocks.transpose(1, 0, 2).reshape(images, width)
    return (correlation, backward(grad_a_n, norm_a, inverse_a), backward(grad_b_n, norm_b, inverse_b))
```

```python
import jax
import jax.numpy as jnp
from jax import lax
from jax.sharding import Mesh, PartitionSpec as P

epsilon = 1e-05
off_weight = 0.005
f32 = jnp.float32
bf16 = jnp.bfloat16
AXES = ("zl", "y", "c", "zh", "x")
DP = ("zl", "y", "c")
FEAT = ("zh", "x")


def exchange(values, axis):
    return lax.all_to_all(values, axis, split_axis=0, concat_axis=0, tiled=False)


def split_halves(values):
    upper = values.astype(bf16)
    lower = (values - upper.astype(f32)).astype(bf16)
    return upper, lower


def dot(left, right, contract):
    return lax.dot_general(left, right, (contract, ((), ())), preferred_element_type=f32)


def standardize(values):
    images = values.shape[0]
    as_float = values.astype(f32)
    mean = jnp.sum(as_float, 0) / images
    inverse = lax.rsqrt(jnp.sum(as_float * as_float, 0) / images - mean * mean + epsilon)
    return ((as_float - mean) * inverse).astype(bf16), mean, inverse


def local(view_a, view_b):
    nz, ny, nc = (lax.axis_size(a) for a in DP)
    nh, nx = (lax.axis_size(a) for a in FEAT)
    rows, cols_a = view_a.shape
    width = view_b.shape[1]
    cols_b = width // (nz * ny * nc)
    images = rows * nz * ny * nc
    iz, iy, ic = (lax.axis_index(a) for a in DP)
    ih, ix = (lax.axis_index(a) for a in FEAT)
    feat = ih * nx + ix

    with jax.named_scope("gather_z"):
        part = width // nz
        send = jnp.concatenate(
            [
                jnp.broadcast_to(view_a[None], (nz, rows, cols_a)),
                view_b.reshape(rows, nz, part).transpose(1, 0, 2),
            ],
            2,
        )
        got = exchange(send, "zl").reshape(nz * rows, cols_a + part)
    with jax.named_scope("gather_y"):
        part = part // ny
        send = jnp.concatenate(
            [
                jnp.broadcast_to(got[None, :, :cols_a], (ny, nz * rows, cols_a)),
                got[:, cols_a:].reshape(nz * rows, ny, part).transpose(1, 0, 2),
            ],
            2,
        )
        got = exchange(send, "y").reshape(ny * nz * rows, cols_a + part)
    with jax.named_scope("gather_core"):
        part = part // nc
        send = jnp.concatenate(
            [
                jnp.broadcast_to(got[None, :, :cols_a], (nc, images // nc, cols_a)),
                got[:, cols_a:].reshape(images // nc, nc, part).transpose(1, 0, 2),
            ],
            2,
        )
        got = exchange(send, "c").reshape(images, cols_a + part)

    with jax.named_scope("tile"):
        norm_a, mean_a, inverse_a = standardize(got[:, :cols_a])
        norm_b, mean_b, inverse_b = standardize(got[:, cols_a:])
        correlation = dot(norm_a, norm_b, ((0,), (0,))) / images
        on_block = (feat == iz).astype(f32)
        first = (iy * nc + ic) * cols_b
        block = lax.dynamic_slice_in_dim(correlation, first, cols_b, 0)
        eye = jnp.eye(cols_b, dtype=f32)
        diagonal = jnp.sum(block * eye, 0)
        shift = -2.0 * (1.0 - diagonal) - 2.0 * off_weight * diagonal
        squares = jnp.sum(correlation * correlation, 1)

    with jax.named_scope("partial_b"):
        upper, lower = split_halves(2.0 * off_weight * correlation)
        part_b = dot(norm_a, upper, ((1,), (0,))) + dot(norm_a, lower, ((1,), (0,)))
        own_a = lax.dynamic_slice_in_dim(norm_a, first, cols_b, 1).astype(f32)
        part_b = part_b + own_a * (shift * on_block)
        float_b = norm_b.astype(f32)
        part_b = (part_b - float_b * jnp.mean(part_b * float_b, 0)) * inverse_b

    with jax.named_scope("sum_b_x"):
        send = part_b.astype(bf16).reshape(nx, images // nx, cols_b)
        sum_b = jnp.sum(exchange(send, "x").astype(f32), 0)

    with jax.named_scope("gram"):
        blocks = nc * ny * nz
        picked = lax.dynamic_index_in_dim(norm_b.reshape(blocks, rows, cols_b), feat, 1, False)
        gram = dot(picked, norm_b, ((1,), (1,)))
        pad = jnp.zeros((cols_b,), f32)
        aux = jnp.concatenate([mean_b, inverse_b, diagonal, pad]).reshape(2, images)
        squares = squares.reshape(-1, images)
        n_sq = squares.shape[0]
    with jax.named_scope("reduce_z"):
        send = jnp.concatenate(
            [
                gram.reshape(nc, ny, nz, images).transpose(2, 1, 0, 3).reshape(nz, ny * nc, images),
                jnp.broadcast_to(squares[None], (nz, n_sq, images)),
                jnp.broadcast_to(aux[None], (nz, 2, images)),
            ],
            1,
        )
        got = exchange(send, "zl")
        total = jnp.sum(got[:, : ny * nc + n_sq], 0)
        aux = lax.dynamic_index_in_dim(got[:, ny * nc + n_sq :], feat, 0, False)
    with jax.named_scope("reduce_yc"):
        send = jnp.concatenate(
            [
                total[: ny * nc, None],
                jnp.broadcast_to(total[None, ny * nc :], (ny * nc, n_sq, images)),
                jnp.broadcast_to(aux[None], (ny * nc, 2, images)),
            ],
            1,
        )
        got = exchange(send, ("y", "c"))
        total = jnp.sum(got[:, : 1 + n_sq], 0)
        gram = total[0]
        squares = total[1:].reshape(cols_a)
        aux = got[:, 1 + n_sq :].reshape(ny * nc, 4, cols_b).transpose(1, 0, 2).reshape(4, cols_a)
        mean_f, inverse_f, diag_f = aux[0], aux[1], aux[2]

    with jax.named_scope("sum_b_zh"):
        upper, lower = split_halves(gram.reshape(2, cols_b))
        own = jnp.concatenate([sum_b.astype(bf16), upper, lower], 0)
        n_rows = images // nx
        got = exchange(jnp.broadcast_to(own[None], (nh,) + own.shape), "zh")
        sum_b = jnp.sum(got[:, :n_rows].astype(f32), 0).astype(bf16)
        gram = got[:, n_rows:].reshape(nh * 4, cols_b)
    with jax.named_scope("gather_b_x"):
        own = jnp.concatenate([sum_b, gram], 0)
        got = exchange(jnp.broadcast_to(own[None], (nx,) + own.shape), "x")
        grad_b = got[:, :n_rows].reshape(nc, ny, nz, rows, cols_b).transpose(2, 1, 0, 3, 4)
        grad_b = grad_b.reshape(images, cols_b).astype(f32)
        gram = got[:, n_rows:].reshape(nx, nh, 2, images).transpose(2, 1, 0, 3).reshape(2, nh * nx, images)

    with jax.named_scope("grad_a"):
        shift = -2.0 * (1.0 - diag_f) - 2.0 * off_weight * diag_f
        projected = 2.0 * off_weight * squares + shift * diag_f
        both = dot(gram.reshape(2 * nh * nx, images), norm_a, ((1,), (0,)))
        scale = 2.0 * off_weight / images
        start_b = view_b_columns(view_b, feat, cols_a)
        own_b = ((start_b - mean_f) * inverse_f).astype(bf16).astype(f32)
        own_a = ((view_a.astype(f32) - mean_a) * inverse_a).astype(bf16).astype(f32)
        grad_a_n = (both[:rows] + both[rows:]) * scale + own_b * shift
        grad_a = (grad_a_n - own_a * projected) * inverse_a
    return correlation, grad_a, grad_b


def view_b_columns(view_b, feat, cols_a):
    return lax.dynamic_slice_in_dim(view_b, feat * cols_a, cols_a, 1).astype(f32)


def solution(mesh):
    sizes = (8, 4, 2, 2, 4)
    fine = Mesh(mesh.devices.reshape(sizes), AXES)
    in_specs = (P(DP, FEAT), P(DP, None))
    out_specs = (P(FEAT, DP), P(DP, FEAT), P(None, DP))
    return jax.shard_map(local, mesh=fine, in_specs=in_specs, out_specs=out_specs, check_vma=False)
```

```python
import jax
import jax.numpy as jnp
from jax import lax
from jax.sharding import Mesh, PartitionSpec as P

epsilon = 1e-05
off_weight = 0.005
f32 = jnp.float32
bf16 = jnp.bfloat16
AXES = ("zl", "y", "c", "zh", "x")
DP = ("zl", "y", "c")
FEAT = ("zh", "x")


def exchange(values, axis):
    return lax.all_to_all(values, axis, split_axis=0, concat_axis=0, tiled=False)


def split_halves(values):
    return terms(values, 2)


def terms(values, count):
    parts = []
    for _ in range(count):
        rounded = lax.reduce_precision(values, 8, 7)
        parts.append(rounded.astype(bf16))
        values = values - rounded
    return parts


def dot(left, right, contract):
    return lax.dot_general(left, right, (contract, ((), ())), preferred_element_type=f32)


def standardize(values):
    images = values.shape[0]
    as_float = values.astype(f32)
    mean = jnp.sum(as_float, 0) / images
    inverse = lax.rsqrt(jnp.sum(as_float * as_float, 0) / images - mean * mean + epsilon)
    return ((as_float - mean) * inverse).astype(bf16), mean, inverse


def local(view_a, view_b):
    nz, ny, nc = (lax.axis_size(a) for a in DP)
    nh, nx = (lax.axis_size(a) for a in FEAT)
    rows, cols_a = view_a.shape
    width = view_b.shape[1]
    cols_b = width // (nz * ny * nc)
    images = rows * nz * ny * nc
    iz, iy, ic = (lax.axis_index(a) for a in DP)
    ih, ix = (lax.axis_index(a) for a in FEAT)
    feat = ih * nx + ix

    with jax.named_scope("gather_z"):
        part = width // nz
        send = jnp.concatenate(
            [
                jnp.broadcast_to(view_a[None], (nz, rows, cols_a)),
                view_b.reshape(rows, nz, part).transpose(1, 0, 2),
            ],
            2,
        )
        got = exchange(send, "zl").reshape(nz * rows, cols_a + part)
    with jax.named_scope("gather_y"):
        part = part // ny
        send = jnp.concatenate(
            [
                jnp.broadcast_to(got[None, :, :cols_a], (ny, nz * rows, cols_a)),
                got[:, cols_a:].reshape(nz * rows, ny, part).transpose(1, 0, 2),
            ],
            2,
        )
        got = exchange(send, "y").reshape(ny * nz * rows, cols_a + part)
    with jax.named_scope("gather_core"):
        part = part // nc
        send = jnp.concatenate(
            [
                jnp.broadcast_to(got[None, :, :cols_a], (nc, images // nc, cols_a)),
                got[:, cols_a:].reshape(images // nc, nc, part).transpose(1, 0, 2),
            ],
            2,
        )
        got = exchange(send, "c").reshape(images, cols_a + part)

    with jax.named_scope("tile"):
        norm_a, mean_a, inverse_a = standardize(got[:, :cols_a])
        norm_b, mean_b, inverse_b = standardize(got[:, cols_a:])
        correlation = dot(norm_a, norm_b, ((0,), (0,))) / images
        on_block = (feat == iz).astype(f32)
        first = (iy * nc + ic) * cols_b
        block = lax.dynamic_slice_in_dim(correlation, first, cols_b, 0)
        eye = jnp.eye(cols_b, dtype=f32)
        diagonal = jnp.sum(block * eye, 0)
        shift = -2.0 * (1.0 - diagonal) - 2.0 * off_weight * diagonal
        squares = jnp.sum(correlation * correlation, 1)

    with jax.named_scope("partial_b"):
        upper, lower = split_halves(2.0 * off_weight * correlation)
        part_b = dot(norm_a, upper, ((1,), (0,))) + dot(norm_a, lower, ((1,), (0,)))
        own_a = lax.dynamic_slice_in_dim(norm_a, first, cols_b, 1).astype(f32)
        part_b = part_b + own_a * (shift * on_block)
        float_b = norm_b.astype(f32)
        part_b = (part_b - float_b * jnp.mean(part_b * float_b, 0)) * inverse_b

    with jax.named_scope("sum_b_x"):
        n_rows = images // nx
        send = part_b.astype(bf16).reshape(nx, n_rows, cols_b)
        sum_b = jnp.sum(exchange(send, "x").astype(f32), 0).astype(bf16)

    with jax.named_scope("gram"):
        take = rows // nx
        n_yc = ny * nc
        picked = lax.dynamic_index_in_dim(norm_b.reshape(images // rows, nx, take, cols_b), ix, 1, False)
        gram = dot(picked.reshape(-1, cols_b), norm_b, ((1,), (1,)))
        gram = gram.reshape(nc, ny, nz, take, images).transpose(2, 1, 0, 3, 4)
        gram = gram.reshape(nz, n_yc * take, images).astype(bf16)
        aux = jnp.concatenate(terms(mean_b, 3) + terms(inverse_b, 3) + terms(diagonal, 2))
        aux = aux.reshape(-1, images)
        squares = squares.reshape(-1, images)
        n_sq, n_aux = squares.shape[0], aux.shape[0]
        n_gram = n_yc * take
    with jax.named_scope("reduce_z"):
        send = jnp.concatenate(
            [
                gram,
                jnp.broadcast_to(squares[None].astype(bf16), (nz, n_sq, images)),
                jnp.broadcast_to(aux[None], (nz, n_aux, images)),
            ],
            1,
        )
        send, sum_b = lax.optimization_barrier((send, sum_b))
        other = lax.ppermute(sum_b, "zh", [(0, 1), (1, 0)])
        got = exchange(send, "zl")
        total = jnp.sum(got[:, : n_gram + n_sq].astype(f32), 0)
        aux = lax.dynamic_index_in_dim(got[:, n_gram + n_sq :], feat, 0, False)
        aux = aux.astype(f32).reshape(-1, cols_b)
        aux = jnp.stack([aux[0] + aux[1] + aux[2], aux[3] + aux[4] + aux[5], aux[6] + aux[7], aux[7]])
        aux = aux.reshape(2, images)
    with jax.named_scope("reduce_yc"):
        send = jnp.concatenate(
            [
                total[:n_gram].reshape(n_yc, take, images),
                jnp.broadcast_to(total[None, n_gram:], (n_yc, n_sq, images)),
                jnp.broadcast_to(aux[None], (n_yc, 2, images)),
            ],
            1,
        )
        got = exchange(send, ("y", "c"))
        total = jnp.sum(got[:, : take + n_sq], 0)
        gram = total[:take]
        squares = total[take:].reshape(cols_a)
        aux = got[:, take + n_sq :].reshape(n_yc, 4, cols_b).transpose(1, 0, 2).reshape(4, cols_a)
        mean_f, inverse_f, diag_f = aux[0], aux[1], aux[2]

    with jax.named_scope("gather_b_x"):
        sum_b = (sum_b.astype(f32) + other.astype(f32)).astype(bf16)
        upper, lower = split_halves(gram)
        own = jnp.concatenate([sum_b, upper.reshape(-1, cols_b), lower.reshape(-1, cols_b)], 0)
        got = exchange(jnp.broadcast_to(own[None], (nx,) + own.shape), "x")
        grad_b = got[:, :n_rows].reshape(nc, ny, nz, rows, cols_b).transpose(2, 1, 0, 3, 4)
        grad_b = grad_b.reshape(images, cols_b).astype(f32)
        gram = got[:, n_rows:].reshape(nx, 2, take, images).transpose(1, 0, 2, 3).reshape(2 * rows, images)

    with jax.named_scope("grad_a"):
        shift = -2.0 * (1.0 - diag_f) - 2.0 * off_weight * diag_f
        projected = 2.0 * off_weight * squares + shift * diag_f
        both = dot(gram, norm_a, ((1,), (0,)))
        scale = 2.0 * off_weight / images
        start_b = view_b_columns(view_b, feat, cols_a)
        own_b = ((start_b - mean_f) * inverse_f).astype(bf16).astype(f32)
        own_a = ((view_a.astype(f32) - mean_a) * inverse_a).astype(bf16).astype(f32)
        grad_a_n = (both[:rows] + both[rows:]) * scale + own_b * shift
        grad_a = (grad_a_n - own_a * projected) * inverse_a
    return correlation, grad_a, grad_b


def view_b_columns(view_b, feat, cols_a):
    return lax.dynamic_slice_in_dim(view_b, feat * cols_a, cols_a, 1).astype(f32)


def solution(mesh):
    sizes = (8, 4, 2, 2, 4)
    fine = Mesh(mesh.devices.reshape(sizes), AXES)
    in_specs = (P(DP, FEAT), P(DP, None))
    out_specs = (P(FEAT, DP), P(DP, FEAT), P(None, DP))
    return jax.shard_map(local, mesh=fine, in_specs=in_specs, out_specs=out_specs, check_vma=False)
```

```python
import jax
import jax.numpy as jnp
from jax import lax
from jax.sharding import Mesh, PartitionSpec as P

epsilon = 1e-05
off_weight = 0.005
f32 = jnp.float32
bf16 = jnp.bfloat16
AXES = ("zl", "y", "c", "zh", "x")
DP = ("zl", "y", "c")
FEAT = ("zh", "x")


def exchange(values, axis):
    return lax.all_to_all(values, axis, split_axis=0, concat_axis=0, tiled=False)


def split_halves(values):
    return terms(values, 2)


def terms(values, count):
    parts = []
    for _ in range(count):
        rounded = lax.reduce_precision(values, 8, 7)
        parts.append(rounded.astype(bf16))
        values = values - rounded
    return parts


def dot(left, right, contract):
    return lax.dot_general(left, right, (contract, ((), ())), preferred_element_type=f32)


def standardize(values):
    images = values.shape[0]
    as_float = values.astype(f32)
    mean = jnp.sum(as_float, 0) / images
    inverse = lax.rsqrt(jnp.sum(as_float * as_float, 0) / images - mean * mean + epsilon)
    return ((as_float - mean) * inverse).astype(bf16), mean, inverse


def local(view_a, view_b):
    nz, ny, nc = (lax.axis_size(a) for a in DP)
    nh, nx = (lax.axis_size(a) for a in FEAT)
    rows, cols_a = view_a.shape
    width = view_b.shape[1]
    cols_b = width // (nz * ny * nc)
    images = rows * nz * ny * nc
    iz, iy, ic = (lax.axis_index(a) for a in DP)
    ih, ix = (lax.axis_index(a) for a in FEAT)
    feat = ih * nx + ix

    with jax.named_scope("gather_z"):
        lanes = cols_b // (nx // nc)
        quarter = view_b.reshape(rows, nz * ny, nx, lanes)
        quarter = lax.dynamic_index_in_dim(quarter, ix, 2, False).reshape(rows, nz, ny * lanes)
        send = jnp.concatenate(
            [jnp.broadcast_to(view_a[None], (nz, rows, cols_a)), quarter.transpose(1, 0, 2)], 2
        )
        got = exchange(send, "zl").reshape(nz * rows, cols_a + ny * lanes)
    with jax.named_scope("gather_y"):
        send = jnp.concatenate(
            [
                jnp.broadcast_to(got[None, :, :cols_a], (ny, nz * rows, cols_a)),
                got[:, cols_a:].reshape(nz * rows, ny, lanes).transpose(1, 0, 2),
            ],
            2,
        )
        got = exchange(send, "y").reshape(ny * nz * rows, cols_a + lanes)
    with jax.named_scope("gather_core"):
        got = exchange(jnp.broadcast_to(got[None], (nc,) + got.shape), "c")
        got = got.reshape(images, cols_a + lanes)
    with jax.named_scope("gather_b_x_raw"):
        part = exchange(jnp.broadcast_to(got[None, :, cols_a:], (nx, images, lanes)), "x")
        part = lax.dynamic_index_in_dim(part.reshape(nc, nx // nc, images, lanes), ic, 0, False)
        raw_b = jnp.concatenate([part[k] for k in range(nx // nc)], 1)

    with jax.named_scope("tile"):
        norm_a, mean_a, inverse_a = standardize(got[:, :cols_a])
        norm_b, mean_b, inverse_b = standardize(raw_b)
        correlation = dot(norm_a, norm_b, ((0,), (0,))) / images
        on_block = (feat == iz).astype(f32)
        first = (iy * nc + ic) * cols_b
        block = lax.dynamic_slice_in_dim(correlation, first, cols_b, 0)
        eye = jnp.eye(cols_b, dtype=f32)
        diagonal = jnp.sum(block * eye, 0)
        shift = -2.0 * (1.0 - diagonal) - 2.0 * off_weight * diagonal
        squares = jnp.sum(correlation * correlation, 1)

    with jax.named_scope("partial_b"):
        upper, lower = split_halves(2.0 * off_weight * correlation)
        part_b = dot(norm_a, upper, ((1,), (0,))) + dot(norm_a, lower, ((1,), (0,)))
        own_a = lax.dynamic_slice_in_dim(norm_a, first, cols_b, 1).astype(f32)
        part_b = part_b + own_a * (shift * on_block)
        float_b = norm_b.astype(f32)
        part_b = (part_b - float_b * jnp.mean(part_b * float_b, 0)) * inverse_b

    with jax.named_scope("sum_b_x"):
        n_rows = images // nx
        send = part_b.astype(bf16).reshape(nx, n_rows, cols_b)
        sum_b = jnp.sum(exchange(send, "x").astype(f32), 0).astype(bf16)

    with jax.named_scope("gram"):
        take = rows // nx
        n_yc = ny * nc
        picked = lax.dynamic_index_in_dim(norm_b.reshape(images // rows, nx, take, cols_b), ix, 1, False)
        gram = dot(picked.reshape(-1, cols_b), norm_b, ((1,), (1,)))
        gram = gram.reshape(nc, ny, nz, take, images).transpose(2, 1, 0, 3, 4)
        gram = gram.reshape(nz, n_yc * take, images).astype(bf16)
        aux = jnp.concatenate(terms(mean_b, 3) + terms(inverse_b, 3) + terms(diagonal, 2))
        aux = aux.reshape(-1, images)
        squares = squares.reshape(-1, images)
        n_sq, n_aux = squares.shape[0], aux.shape[0]
        n_gram = n_yc * take
    with jax.named_scope("reduce_z"):
        send = jnp.concatenate(
            [
                gram,
                jnp.broadcast_to(squares[None].astype(bf16), (nz, n_sq, images)),
                jnp.broadcast_to(aux[None], (nz, n_aux, images)),
            ],
            1,
        )
        send, sum_b = lax.optimization_barrier((send, sum_b))
        other = lax.ppermute(sum_b, "zh", [(0, 1), (1, 0)])
        got = exchange(send, "zl")
        total = jnp.sum(got[:, : n_gram + n_sq].astype(f32), 0)
        aux = lax.dynamic_index_in_dim(got[:, n_gram + n_sq :], feat, 0, False)
        aux = aux.astype(f32).reshape(-1, cols_b)
        aux = jnp.stack([aux[0] + aux[1] + aux[2], aux[3] + aux[4] + aux[5], aux[6] + aux[7], aux[7]])
        aux = aux.reshape(2, images)
    with jax.named_scope("reduce_yc"):
        send = jnp.concatenate(
            [
                total[:n_gram].reshape(n_yc, take, images),
                jnp.broadcast_to(total[None, n_gram:], (n_yc, n_sq, images)),
                jnp.broadcast_to(aux[None], (n_yc, 2, images)),
            ],
            1,
        )
        got = exchange(send, ("y", "c"))
        total = jnp.sum(got[:, : take + n_sq], 0)
        gram = total[:take]
        squares = total[take:].reshape(cols_a)
        aux = got[:, take + n_sq :].reshape(n_yc, 4, cols_b).transpose(1, 0, 2).reshape(4, cols_a)
        mean_f, inverse_f, diag_f = aux[0], aux[1], aux[2]

    with jax.named_scope("shift_a"):
        shift = -2.0 * (1.0 - diag_f) - 2.0 * off_weight * diag_f
        projected = 2.0 * off_weight * squares + shift * diag_f
        own_b = ((view_b_columns(view_b, feat, cols_a) - mean_f) * inverse_f).astype(bf16).astype(f32)
        own_a = ((view_a.astype(f32) - mean_a) * inverse_a).astype(bf16).astype(f32)
        shifted = (own_b * shift - own_a * projected) * inverse_a
        scale = jnp.broadcast_to(2.0 * off_weight / images * inverse_a, (rows, cols_a))
    with jax.named_scope("gather_b_x"):
        sum_b = (sum_b.astype(f32) + other.astype(f32)).astype(bf16)
        upper, lower = terms(gram, 2)
        own = jnp.concatenate([sum_b, upper.reshape(-1, cols_b), lower.reshape(-1, cols_b)], 0)
        own, shifted, scale = lax.optimization_barrier((own, shifted, scale))
        got = exchange(jnp.broadcast_to(own[None], (nx,) + own.shape), "x")
        grad_b = got[:, :n_rows].reshape(nc, ny, nz, rows, cols_b).transpose(2, 1, 0, 3, 4)
        grad_b = grad_b.reshape(images, cols_b).astype(f32)
        gram = got[:, n_rows:].reshape(nx, 2, take, images).transpose(1, 0, 2, 3).reshape(2 * rows, images)
    with jax.named_scope("grad_a"):
        both = dot(gram, norm_a, ((1,), (0,)))
        grad_a = (both[:rows] + both[rows:]) * scale + shifted
    return correlation, grad_a, grad_b


def view_b_columns(view_b, feat, cols_a):
    return lax.dynamic_slice_in_dim(view_b, feat * cols_a, cols_a, 1).astype(f32)


def solution(mesh):
    sizes = (8, 4, 2, 2, 4)
    fine = Mesh(mesh.devices.reshape(sizes), AXES)
    in_specs = (P(DP, FEAT), P(DP, None))
    out_specs = (P(FEAT, DP), P(DP, FEAT), P(None, DP))
    return jax.shard_map(local, mesh=fine, in_specs=in_specs, out_specs=out_specs, check_vma=False)
```

```python
import functools
import jax
import jax.numpy as jnp
from jax import lax
from jax.experimental import pallas as pl
from jax.experimental.pallas import tpu as pltpu
from jax.sharding import Mesh, PartitionSpec as P

epsilon = 1e-05
off_weight = 0.005
f32 = jnp.float32
bf16 = jnp.bfloat16
AXES = ("zl", "y", "c", "zh", "x")
DP = ("zl", "y", "c")
FEAT = ("zh", "x")
SWAP = [(0, 1), (1, 0)]
VMEM_LIMIT = 40 * 1024 * 1024


def exchange(values, axis):
    return lax.all_to_all(values, axis, split_axis=0, concat_axis=0, tiled=False)


def terms(values, count):
    parts = []
    for _ in range(count):
        rounded = lax.reduce_precision(values, 8, 7)
        parts.append(rounded.astype(bf16))
        values = values - rounded
    return parts


def kernel_terms(values, count):
    parts = []
    for _ in range(count):
        parts.append(values.astype(bf16).astype(f32))
        values = values - parts[-1]
    return parts


def dot(left, right, contract):
    return lax.dot_general(left, right, (contract, ((), ())), preferred_element_type=f32)


def statistics(total, square, images):
    mean = total / images
    return mean, lax.rsqrt(square / images - mean * mean + epsilon)


def standardize_kernel(idx, own_ref, other_ref, norm_ref, stat_ref):
    half = own_ref.shape[0]
    cols = norm_ref.shape[1]
    own_place = pl.multiple_of(idx[0] * half, half)
    other_place = pl.multiple_of((1 - idx[0]) * half, half)
    block = 256
    for j in range(cols // block):
        span = slice(j * block, (j + 1) * block)
        own = own_ref[:, span].astype(f32)
        other = other_ref[:, span].astype(f32)
        total = jnp.sum(own, 0, keepdims=True) + jnp.sum(other, 0, keepdims=True)
        square = jnp.sum(own * own, 0, keepdims=True) + jnp.sum(other * other, 0, keepdims=True)
        mean, inverse = statistics(total, square, 2 * half)
        norm_ref[pl.ds(own_place, half), span] = ((own - mean) * inverse).astype(bf16)
        norm_ref[pl.ds(other_place, half), span] = ((other - mean) * inverse).astype(bf16)
        stat_ref[0:1, span] = mean
        stat_ref[1:2, span] = inverse


def in_vmem(count):
    return [pl.BlockSpec(memory_space=pltpu.VMEM)] * count


def standardize_a(idx, own, other, cols):
    half = own.shape[0]
    return pl.pallas_call(
        standardize_kernel,
        out_shape=(
            jax.ShapeDtypeStruct((2 * half, cols), bf16),
            jax.ShapeDtypeStruct((8, cols), f32),
        ),
        in_specs=[pl.BlockSpec(memory_space=pltpu.SMEM)] + in_vmem(2),
        out_specs=in_vmem(2),
        compiler_params=pltpu.CompilerParams(vmem_limit_bytes=VMEM_LIMIT),
        cost_estimate=pl.CostEstimate(
            flops=20 * half * cols, bytes_accessed=8 * half * cols, transcendentals=cols
        ),
    )(idx, own, other)


def tile_kernel(nz, ny, nc, nx, idx, a_ref, b_ref, corr_ref, part_ref, send_ref, norm_ref, high, low, tail):
    images, cols = norm_ref.shape
    cols_a = a_ref.shape[1]
    half, lanes = b_ref.shape[-2:]
    rows = images // (nz * ny * nc)
    take = rows // nx

    for h in range(cols // lanes):
        span = slice(h * lanes, (h + 1) * lanes)
        values = [b_ref[c, idx[0], h].astype(f32) for c in range(nc)]
        total = sum(jnp.sum(v, 0, keepdims=True) for v in values)
        square = sum(jnp.sum(v * v, 0, keepdims=True) for v in values)
        mean, inverse = statistics(total, square, images)
        for c in range(nc):
            norm_ref[c * half : (c + 1) * half, span] = ((values[c] - mean) * inverse).astype(bf16)
        for k, part in enumerate(kernel_terms(mean, 3) + kernel_terms(inverse, 3)):
            tail[8 + k : 9 + k, span] = part
        tail[16:17, span] = inverse

    norm = norm_ref[...]
    ones = jnp.ones((8, cols), bf16)
    for j in range(cols_a // cols):
        span = slice(j * cols, (j + 1) * cols)
        corr = dot(a_ref[:, span], norm, ((0,), (0,))) / images
        corr_ref[span, :] = corr
        upper, lower = (v.astype(bf16) for v in kernel_terms(corr * corr, 2))
        sums = dot(ones, upper, ((1,), (1,))) + dot(ones, lower, ((1,), (1,)))
        tail[j : j + 1, :] = sums[0:1]
        upper, lower = kernel_terms(2.0 * off_weight * corr, 2)
        high[span, :] = upper.astype(bf16)
        low[span, :] = lower.astype(bf16)

    picks = nz * ny * nc * take
    out = lax.broadcasted_iota(jnp.int32, (picks, images), 0)
    image = lax.broadcasted_iota(jnp.int32, (picks, images), 1)
    t, c, y, z = out & 1, (out >> 1) & 1, (out >> 2) & 3, out >> 4
    wanted = ((c * ny + y) * nz + z) * rows + idx[1] * take + t
    select = jnp.where(image == wanted, 1.0, 0.0).astype(bf16)
    picked = dot(select, norm, ((1,), (0,))).astype(bf16)
    gram = dot(picked, norm, ((1,), (1,)))
    for z in range(nz):
        send_ref[z, :, :images] = gram[z * 16 : z * 16 + 16].astype(bf16)

    place = pl.multiple_of(idx[2] * cols, cols)
    corr = corr_ref[pl.ds(place, cols), :]
    row = lax.broadcasted_iota(jnp.int32, corr.shape, 0)
    col = lax.broadcasted_iota(jnp.int32, corr.shape, 1)
    diagonal = jnp.sum(jnp.where(row == col, corr, 0.0), 0, keepdims=True)
    for k, part in enumerate(kernel_terms(diagonal, 2)):
        tail[14 + k : 15 + k, :] = part
    values = tail[0:16, :].astype(bf16)
    for z in range(nz):
        send_ref[z, :, images:] = values

    shift = -2.0 * (1.0 - diagonal) - 2.0 * off_weight * diagonal
    shift = jnp.where(idx[3] == 1, shift, 0.0)
    chunk = images // nx
    totals = []
    for k in range(nx):
        span = slice(k * chunk, (k + 1) * chunk)
        total = dot(a_ref[span, :], high[...], ((1,), (0,))) + dot(a_ref[span, :], low[...], ((1,), (0,)))
        totals.append(total + a_ref[span, pl.ds(place, cols)].astype(f32) * shift)
    along = 0.0
    for k in range(nx):
        along += jnp.sum(totals[k] * norm_ref[k * chunk : (k + 1) * chunk, :].astype(f32), 0, keepdims=True)
    along = along / images
    for k in range(nx):
        total = totals[k] - norm_ref[k * chunk : (k + 1) * chunk, :].astype(f32) * along
        to = lax.rem(k + nx - idx[1], nx)
        part_ref[pl.ds(pl.multiple_of(to * chunk, chunk), chunk), :] = (total * tail[16:17, :]).astype(bf16)


def tile(idx, norm_a, parts, sizes):
    nz, ny, nc, nx = sizes
    images, cols_a = norm_a.shape
    halves, half, lanes = parts.shape[2:]
    cols = halves * lanes
    return pl.pallas_call(
        functools.partial(tile_kernel, nz, ny, nc, nx),
        out_shape=(
            jax.ShapeDtypeStruct((cols_a, cols), f32),
            jax.ShapeDtypeStruct((images, cols), bf16),
            jax.ShapeDtypeStruct((nz, 16, images + cols), bf16),
        ),
        in_specs=[pl.BlockSpec(memory_space=pltpu.SMEM)] + in_vmem(2),
        out_specs=in_vmem(3),
        scratch_shapes=[
            pltpu.VMEM((images, cols), bf16),
            pltpu.VMEM((cols_a, cols), bf16),
            pltpu.VMEM((cols_a, cols), bf16),
            pltpu.VMEM((24, cols), f32),
        ],
        compiler_params=pltpu.CompilerParams(vmem_limit_bytes=VMEM_LIMIT),
        cost_estimate=pl.CostEstimate(
            flops=6 * images * cols_a * cols, bytes_accessed=4 * images * cols_a, transcendentals=0
        ),
    )(idx, norm_a, parts)


def local(view_a, view_b):
    nz, ny, nc = (lax.axis_size(a) for a in DP)
    nh, nx = (lax.axis_size(a) for a in FEAT)
    rows, cols_a = view_a.shape
    width = view_b.shape[1]
    cols_b = width // (nz * ny * nc)
    images = rows * nz * ny * nc
    iz, iy, ic = (lax.axis_index(a) for a in DP)
    ih, ix = (lax.axis_index(a) for a in FEAT)
    feat = ih * nx + ix
    n_yc = ny * nc

    with jax.named_scope("gather_z"):
        lanes = cols_b // (nx // nc)
        quarter = view_b.reshape(rows, nz * ny, nx, lanes)
        quarter = lax.dynamic_index_in_dim(quarter, ix, 2, False).reshape(rows, nz, ny * lanes)
        send = jnp.concatenate(
            [jnp.broadcast_to(view_a[None], (nz, rows, cols_a)), quarter.transpose(1, 0, 2)], 2
        )
        got = exchange(send, "zl").reshape(nz * rows, cols_a + ny * lanes)
    with jax.named_scope("gather_y"):
        send = jnp.concatenate(
            [
                jnp.broadcast_to(got[None, :, :cols_a], (ny, nz * rows, cols_a)),
                got[:, cols_a:].reshape(nz * rows, ny, lanes).transpose(1, 0, 2),
            ],
            2,
        )
        got = exchange(send, "y").reshape(ny * nz * rows, cols_a + lanes)
    with jax.named_scope("gather_core_x"):
        got_other = lax.ppermute(got, "c", SWAP)
        half = images // nc
        parts = exchange(jnp.broadcast_to(got[None, :, cols_a:], (nc * nx, half, lanes)), ("c", "x"))
        parts = parts.reshape(nc, nc, nx // nc, half, lanes)
    with jax.named_scope("standardize_a"):
        idx = jnp.stack([ic, ix, iy * nc + ic, (feat == iz).astype(jnp.int32)]).astype(jnp.int32)
        norm_a, stat_a = standardize_a(idx, got, got_other, cols_a)
        norm_a, parts = lax.optimization_barrier((norm_a, parts))
        mean_a, inverse_a = stat_a[0], stat_a[1]
    with jax.named_scope("tile"):
        correlation, part_b, send = tile(idx, norm_a, parts, (nz, ny, nc, nx))

    with jax.named_scope("reduce_z"):
        got = exchange(send, "zl")
    with jax.named_scope("sum_b_x"):
        n_rows = images // nx
        pieces = [part_b[:n_rows]]
        for k in range(1, nx):
            perm = [(i, (i + k) % nx) for i in range(nx)]
            pieces.append(lax.ppermute(part_b[k * n_rows : (k + 1) * n_rows], "x", perm))
        sum_b = sum(p.astype(f32) for p in pieces).astype(bf16)
        other = lax.ppermute(sum_b, "zh", SWAP)
    with jax.named_scope("reduce_yc"):
        take = rows // nx
        total = jnp.sum(got[:, :, :images].astype(f32), 0).reshape(n_yc, take * images // cols_b, cols_b)
        squares = jnp.sum(got[:, :8, images:].astype(f32), 0)
        aux = lax.dynamic_index_in_dim(got[:, 8:, images:], feat, 0, False).astype(f32)
        aux = jnp.stack([aux[0] + aux[1] + aux[2], aux[3] + aux[4] + aux[5], aux[6] + aux[7], aux[7]])
        right = jnp.concatenate([total, jnp.broadcast_to(aux[None], (n_yc, 4, cols_b))], 1)
        send = jnp.concatenate([jnp.broadcast_to(squares[None], (n_yc, 8, cols_b)), right], 2)
        got = exchange(send, ("y", "c"))
        squares = jnp.sum(got[:, :, :cols_b], 0).reshape(cols_a)
        gram = jnp.sum(got[:, :4, cols_b:], 0)
        mean_f, inverse_f, diag_f = (got[:, 4 + k, cols_b:].reshape(cols_a) for k in range(3))

    with jax.named_scope("shift_a"):
        shift = -2.0 * (1.0 - diag_f) - 2.0 * off_weight * diag_f
        projected = 2.0 * off_weight * squares + shift * diag_f
        own_b = ((view_b_columns(view_b, feat, cols_a) - mean_f) * inverse_f).astype(bf16).astype(f32)
        own_a = ((view_a.astype(f32) - mean_a) * inverse_a).astype(bf16).astype(f32)
        shifted = (own_b * shift - own_a * projected) * inverse_a
        scale = jnp.broadcast_to(2.0 * off_weight / images * inverse_a, (rows, cols_a))
    with jax.named_scope("gather_b_x"):
        sum_b = (sum_b.astype(f32) + other.astype(f32)).astype(bf16)
        upper, lower = terms(gram, 2)
        own = jnp.concatenate([sum_b, upper, lower], 0)
        shifted, scale = lax.optimization_barrier((shifted, scale))
        got = exchange(jnp.broadcast_to(own[None], (nx,) + own.shape), "x")
        grad_b = got[:, :n_rows].reshape(nc, ny, nz, rows, cols_b).transpose(2, 1, 0, 3, 4)
        grad_b = grad_b.reshape(images, cols_b).astype(f32)
        gram = got[:, n_rows:].reshape(nx, 2, take, images).transpose(1, 0, 2, 3).reshape(2 * rows, images)
    with jax.named_scope("grad_a"):
        both = dot(gram, norm_a, ((1,), (0,)))
        grad_a = (both[:rows] + both[rows:]) * scale + shifted
    return correlation, grad_a, grad_b


def view_b_columns(view_b, feat, cols_a):
    return lax.dynamic_slice_in_dim(view_b, feat * cols_a, cols_a, 1).astype(f32)


def solution(mesh):
    sizes = (8, 4, 2, 2, 4)
    fine = Mesh(mesh.devices.reshape(sizes), AXES)
    in_specs = (P(DP, FEAT), P(DP, None))
    out_specs = (P(FEAT, DP), P(DP, FEAT), P(None, DP))
    return jax.shard_map(local, mesh=fine, in_specs=in_specs, out_specs=out_specs, check_vma=False)
```

```python
import functools
import jax
import jax.numpy as jnp
from jax import lax
from jax.experimental import pallas as pl
from jax.experimental.pallas import tpu as pltpu
from jax.sharding import Mesh, PartitionSpec as P

epsilon = 1e-05
off_weight = 0.005
f32 = jnp.float32
bf16 = jnp.bfloat16
AXES = ("zl", "y", "c", "zh", "x")
DP = ("zl", "y", "c")
FEAT = ("zh", "x")
SWAP = [(0, 1), (1, 0)]
VMEM_LIMIT = 14 * 1024 * 1024


def exchange(values, axis):
    return lax.all_to_all(values, axis, split_axis=0, concat_axis=0, tiled=False)


def terms(values, count):
    parts = []
    for _ in range(count):
        rounded = lax.reduce_precision(values, 8, 7)
        parts.append(rounded.astype(bf16))
        values = values - rounded
    return parts


def kernel_terms(values, count):
    parts = []
    for _ in range(count):
        parts.append(values.astype(bf16).astype(f32))
        values = values - parts[-1]
    return parts


def dot(left, right, contract):
    return lax.dot_general(left, right, (contract, ((), ())), preferred_element_type=f32)


def statistics(total, square, images):
    mean = total / images
    return mean, lax.rsqrt(square / images - mean * mean + epsilon)


def pack_kernel(ny, nc, idx, a_hbm, b_hbm, send_ref, a_ref, b_ref, sems):
    nz, rows, _ = send_ref.shape
    cols_a = a_ref.shape[1]
    copy_a = pltpu.make_async_copy(a_hbm, a_ref, sems.at[0])
    copy_b = pltpu.make_async_copy(b_hbm, b_ref, sems.at[1])
    copy_b.start()
    copy_a.start()
    copy_a.wait()
    values = a_ref[...]
    for z in range(nz):
        send_ref[z, :, :cols_a] = values
    copy_b.wait()
    lanes = (send_ref.shape[2] - cols_a) // ny
    upper = idx[1] < 2
    column = (idx[1] & 1) * lanes
    keep = (lax.broadcasted_iota(jnp.int32, (rows, lanes), 0) < rows // 2) == upper
    for z in range(nz):
        for y in range(ny):
            pair = []
            for c in range(nc):
                first = ((z * ny + y) * nc + c) * 2 * lanes
                first = pl.multiple_of(first + column, lanes)
                pair.append(b_ref[:, pl.ds(first, lanes)].astype(f32))
            moved = pltpu.roll(jnp.where(upper, pair[1], pair[0]), rows // 2, 0)
            mixed = jnp.where(keep, jnp.where(upper, pair[0], pair[1]), moved)
            send_ref[z, :, cols_a + y * lanes : cols_a + (y + 1) * lanes] = mixed.astype(bf16)


def pack(idx, view_a, view_b, sizes):
    nz, ny, nc, nx = sizes
    rows, cols_a = view_a.shape
    lanes = view_b.shape[1] // (nz * ny * nc * 2)
    return pl.pallas_call(
        functools.partial(pack_kernel, ny, nc),
        out_shape=jax.ShapeDtypeStruct((nz, rows, cols_a + ny * lanes), bf16),
        in_specs=[pl.BlockSpec(memory_space=pltpu.SMEM)] + [pl.BlockSpec(memory_space=pl.ANY)] * 2,
        out_specs=in_vmem(1)[0],
        scratch_shapes=[
            pltpu.VMEM(view_a.shape, bf16),
            pltpu.VMEM(view_b.shape, bf16),
            pltpu.SemaphoreType.DMA((2,)),
        ],
        compiler_params=pltpu.CompilerParams(vmem_limit_bytes=VMEM_LIMIT),
    )(idx, view_a, view_b)


def standardize_kernel(idx, own_ref, other_ref, norm_ref, stat_ref):
    half = own_ref.shape[0]
    cols = norm_ref.shape[1]
    own_place = pl.multiple_of(idx[0] * half, half)
    other_place = pl.multiple_of((1 - idx[0]) * half, half)
    block = 256
    for j in range(cols // block):
        span = slice(j * block, (j + 1) * block)
        own = own_ref[:, span].astype(f32)
        other = other_ref[:, span].astype(f32)
        total = jnp.sum(own, 0, keepdims=True) + jnp.sum(other, 0, keepdims=True)
        square = jnp.sum(own * own, 0, keepdims=True) + jnp.sum(other * other, 0, keepdims=True)
        mean, inverse = statistics(total, square, 2 * half)
        norm_ref[pl.ds(own_place, half), span] = ((own - mean) * inverse).astype(bf16)
        norm_ref[pl.ds(other_place, half), span] = ((other - mean) * inverse).astype(bf16)
        stat_ref[0:1, span] = mean
        stat_ref[1:2, span] = inverse


def in_vmem(count):
    return [pl.BlockSpec(memory_space=pltpu.VMEM)] * count


def standardize_a(idx, own, other, cols):
    half = own.shape[0]
    return pl.pallas_call(
        standardize_kernel,
        out_shape=(
            jax.ShapeDtypeStruct((2 * half, cols), bf16),
            jax.ShapeDtypeStruct((8, cols), f32),
        ),
        in_specs=[pl.BlockSpec(memory_space=pltpu.SMEM)] + in_vmem(2),
        out_specs=in_vmem(2),
        compiler_params=pltpu.CompilerParams(vmem_limit_bytes=VMEM_LIMIT),
        cost_estimate=pl.CostEstimate(
            flops=20 * half * cols, bytes_accessed=8 * half * cols, transcendentals=cols
        ),
    )(idx, own, other)


def tile_kernel(
    nz, ny, nc, nx, idx, a_ref, b_ref, out_ref, part_ref, norm_ref, tail, corr_ref, high, sems
):
    images, cols = norm_ref.shape
    cols_a = a_ref.shape[1]
    part, lanes = b_ref.shape[-2:]
    parts = b_ref.shape[1]
    half = part * parts
    rows = images // (nz * ny * nc)

    deep = part // rows
    keep = lax.broadcasted_iota(jnp.int32, (deep, rows, lanes), 1) < rows // 2
    for h in range(cols // lanes):
        span = slice(h * lanes, (h + 1) * lanes)
        values = [b_ref[c, k, h].astype(f32) for c in range(nc) for k in range(parts)]
        total = sum(jnp.sum(v, 0, keepdims=True) for v in values)
        square = sum(jnp.sum(v * v, 0, keepdims=True) for v in values)
        mean, inverse = statistics(total, square, images)
        values = [((v - mean) * inverse).reshape(deep, rows, lanes) for v in values]
        for c in range(nc):
            first, second = values[2 * c], values[2 * c + 1]
            even = jnp.where(keep, first, pltpu.roll(second, rows // 2, 1))
            odd = jnp.where(keep, pltpu.roll(first, rows // 2, 1), second)
            norm_ref[c * half : (c + 1) * half, span] = jnp.stack([even, odd], 1).reshape(half, lanes).astype(bf16)
        for k, term in enumerate(kernel_terms(mean, 3) + kernel_terms(inverse, 3)):
            tail[8 + k : 9 + k, span] = term
        tail[16:17, span] = inverse

    norm = norm_ref[...]
    ones = jnp.ones((8, cols), bf16)
    copies = []
    for j in range(cols_a // cols):
        span = slice(j * cols, (j + 1) * cols)
        corr = dot(a_ref[:, span], norm, ((0,), (0,))) / images
        corr_ref[span, :] = corr
        place = pl.ds(j * cols, cols)
        copies.append(pltpu.make_async_copy(corr_ref.at[place], out_ref.at[place], sems.at[j]))
        copies[-1].start()
        upper, lower = (v.astype(bf16) for v in kernel_terms(corr * corr, 2))
        sums = dot(ones, upper, ((1,), (1,))) + dot(ones, lower, ((1,), (1,)))
        tail[j : j + 1, :] = sums[0:1]
        high[span, :] = corr.astype(bf16)

    place = pl.multiple_of(idx[2] * cols, cols)
    corr = corr_ref[pl.ds(place, cols), :]
    row = lax.broadcasted_iota(jnp.int32, corr.shape, 0)
    col = lax.broadcasted_iota(jnp.int32, corr.shape, 1)
    diagonal = jnp.sum(jnp.where(row == col, corr, 0.0), 0, keepdims=True)
    for k, part in enumerate(kernel_terms(diagonal, 2)):
        tail[14 + k : 15 + k, :] = part
    shift = -2.0 * (1.0 - diagonal) - 2.0 * off_weight * diagonal
    shift = jnp.where(idx[3] == 1, shift, 0.0)
    chunk = images // nx
    totals = []
    for k in range(nx):
        span = slice(k * chunk, (k + 1) * chunk)
        total = dot(a_ref[span, :], high[...], ((1,), (0,))) * (2.0 * off_weight)
        totals.append(total + a_ref[span, pl.ds(place, cols)].astype(f32) * shift)
    along = 0.0
    for k in range(nx):
        along += jnp.sum(totals[k] * norm_ref[k * chunk : (k + 1) * chunk, :].astype(f32), 0, keepdims=True)
    along = along / images
    for k in range(nx):
        total = totals[k] - norm_ref[k * chunk : (k + 1) * chunk, :].astype(f32) * along
        to = k ^ idx[1]
        to = to ^ (to >> 1)
        part_ref[pl.ds(pl.multiple_of(to * chunk, chunk), chunk), :] = (total * tail[16:17, :]).astype(bf16)
    for copy in copies:
        copy.wait()


def tile(idx, norm_a, parts, sizes):
    nz, ny, nc, nx = sizes
    images, cols_a = norm_a.shape
    cols = parts.shape[2] * parts.shape[4]
    return pl.pallas_call(
        functools.partial(tile_kernel, nz, ny, nc, nx),
        out_shape=(
            jax.ShapeDtypeStruct((cols_a, cols), f32),
            jax.ShapeDtypeStruct((images, cols), bf16),
            jax.ShapeDtypeStruct((images, cols), bf16),
            jax.ShapeDtypeStruct((24, cols), f32),
        ),
        in_specs=[pl.BlockSpec(memory_space=pltpu.SMEM)] + in_vmem(2),
        out_specs=[pl.BlockSpec(memory_space=pl.ANY)] + in_vmem(3),
        scratch_shapes=[
            pltpu.VMEM((cols_a, cols), f32),
            pltpu.VMEM((cols_a, cols), bf16),
            pltpu.SemaphoreType.DMA((cols_a // cols,)),
        ],
        compiler_params=pltpu.CompilerParams(vmem_limit_bytes=VMEM_LIMIT),
        cost_estimate=pl.CostEstimate(
            flops=6 * images * cols_a * cols, bytes_accessed=4 * images * cols_a, transcendentals=0
        ),
    )(idx, norm_a, parts)


def gram_kernel(nz, ny, nc, nx, idx, norm_ref, tail, send_ref):
    images, cols = norm_ref.shape
    rows = images // (nz * ny * nc)
    take = rows // nx
    norm = norm_ref[...]
    picks = nz * ny * nc * take
    out = lax.broadcasted_iota(jnp.int32, (picks, images), 0)
    image = lax.broadcasted_iota(jnp.int32, (picks, images), 1)
    t, c, y, z = out & 1, (out >> 1) & 1, (out >> 2) & 3, out >> 4
    wanted = ((c * ny + y) * nz + z) * rows + idx[1] * take + t
    select = jnp.where(image == wanted, 1.0, 0.0).astype(bf16)
    picked = dot(select, norm, ((1,), (0,))).astype(bf16)
    gram = dot(picked, norm, ((1,), (1,)))
    for z in range(nz):
        send_ref[z, :, :images] = gram[z * 16 : z * 16 + 16].astype(bf16)

    values = tail[0:16, :].astype(bf16)
    for z in range(nz):
        send_ref[z, :, images:] = values


def gram_part(idx, norm_b, tail, sizes):
    nz = sizes[0]
    images, cols = norm_b.shape
    return pl.pallas_call(
        functools.partial(gram_kernel, *sizes),
        out_shape=jax.ShapeDtypeStruct((nz, 16, images + cols), bf16),
        in_specs=[pl.BlockSpec(memory_space=pltpu.SMEM)] + in_vmem(2),
        out_specs=in_vmem(1)[0],
        compiler_params=pltpu.CompilerParams(vmem_limit_bytes=VMEM_LIMIT),
        cost_estimate=pl.CostEstimate(
            flops=8 * images * images * cols, bytes_accessed=16 * images * cols, transcendentals=0
        ),
    )(idx, norm_b, tail)


def local(view_a, view_b):
    nz, ny, nc = (lax.axis_size(a) for a in DP)
    nh, nx = (lax.axis_size(a) for a in FEAT)
    rows, cols_a = view_a.shape
    width = view_b.shape[1]
    cols_b = width // (nz * ny * nc)
    images = rows * nz * ny * nc
    iz, iy, ic = (lax.axis_index(a) for a in DP)
    ih, ix = (lax.axis_index(a) for a in FEAT)
    feat = ih * nx + ix
    n_yc = ny * nc

    with jax.named_scope("gather_z"):
        lanes = cols_b // 2
        idx = jnp.stack([ic, ix, iy * nc + ic, (feat == iz).astype(jnp.int32)]).astype(jnp.int32)
        send = pack(idx, view_a, view_b, (nz, ny, nc, nx))
        got = exchange(send, "zl").reshape(nz * rows, cols_a + ny * lanes)
    with jax.named_scope("gather_y"):
        send = jnp.concatenate(
            [
                jnp.broadcast_to(got[None, :, :cols_a], (ny, nz * rows, cols_a)),
                got[:, cols_a:].reshape(nz * rows, ny, lanes).transpose(1, 0, 2),
            ],
            2,
        )
        got = exchange(send, "y").reshape(ny * nz * rows, cols_a + lanes)
    with jax.named_scope("gather_core_x"):
        got_other = lax.ppermute(got, "c", SWAP)
        half = images // nc
        parts = got[:, cols_a:].reshape(half // rows, nc, rows // nc, lanes).transpose(1, 0, 2, 3)
        parts = parts.reshape(nc, 1, half // nc, lanes)
        parts = jnp.broadcast_to(parts, (nc, nx, half // nc, lanes)).reshape(nc * nx, half // nc, lanes)
        parts = exchange(parts, ("c", "x")).reshape(nc, nx // 2, 2, half // nc, lanes)
    with jax.named_scope("standardize_a"):
        norm_a, stat_a = standardize_a(idx, got, got_other, cols_a)
        norm_a, parts = lax.optimization_barrier((norm_a, parts))
        mean_a, inverse_a = stat_a[0], stat_a[1]
    with jax.named_scope("tile"):
        correlation, part_b, norm_b, tail = tile(idx, norm_a, parts, (nz, ny, nc, nx))

    with jax.named_scope("sum_b_x_reduce_z"):
        n_rows = images // nx
        came = lax.ppermute(part_b[2 * n_rows :], "x", [(i, i ^ 3) for i in range(nx)])
        send = gram_part(idx, norm_b, tail, (nz, ny, nc, nx))
        got = exchange(send, "zl")
        sum_b = part_b[: 2 * n_rows].astype(f32) + came.astype(f32)
        came = lax.ppermute(sum_b[n_rows:].astype(bf16), "x", [(i, i ^ 1) for i in range(nx)])
        sum_b = (sum_b[:n_rows] + came.astype(f32)).astype(bf16)
    with jax.named_scope("reduce_yc"):
        take = rows // nx
        total = jnp.sum(got[:, :, :images].astype(f32), 0).reshape(n_yc, take * images // cols_b, cols_b)
        squares = jnp.sum(got[:, :8, images:].astype(f32), 0)
        aux = lax.dynamic_index_in_dim(got[:, 8:, images:], feat, 0, False).astype(f32)
        aux = jnp.stack([aux[0] + aux[1] + aux[2], aux[3] + aux[4] + aux[5], aux[6] + aux[7], aux[7]])
        right = jnp.concatenate([total, jnp.broadcast_to(aux[None], (n_yc, 4, cols_b))], 1)
        send = jnp.concatenate([jnp.broadcast_to(squares[None], (n_yc, 8, cols_b)), right], 2)
        other = lax.ppermute(sum_b, "zh", SWAP)
        got = exchange(send, ("y", "c"))
        squares = jnp.sum(got[:, :, :cols_b], 0).reshape(cols_a)
        gram = jnp.sum(got[:, :4, cols_b:], 0)
        mean_f, inverse_f, diag_f = (got[:, 4 + k, cols_b:].reshape(cols_a) for k in range(3))

    with jax.named_scope("shift_a"):
        shift = -2.0 * (1.0 - diag_f) - 2.0 * off_weight * diag_f
        projected = 2.0 * off_weight * squares + shift * diag_f
        own_b = ((view_b_columns(view_b, feat, cols_a) - mean_f) * inverse_f).astype(bf16).astype(f32)
        own_a = ((view_a.astype(f32) - mean_a) * inverse_a).astype(bf16).astype(f32)
        shifted = (own_b * shift - own_a * projected) * inverse_a
        scale = jnp.broadcast_to(2.0 * off_weight / images * inverse_a, (rows, cols_a))
    with jax.named_scope("gather_b_x"):
        sum_b = (sum_b.astype(f32) + other.astype(f32)).astype(bf16)
        upper, lower = terms(gram, 2)
        own = jnp.concatenate([sum_b, upper, lower], 0)
        shifted, scale = lax.optimization_barrier((shifted, scale))
        got = exchange(jnp.broadcast_to(own[None], (nx,) + own.shape), "x")
        grad_b = got[:, :n_rows].reshape(nc, ny, nz, rows, cols_b).transpose(2, 1, 0, 3, 4)
        grad_b = grad_b.reshape(images, cols_b).astype(f32)
        gram = got[:, n_rows:].reshape(nx, 2, take, images).transpose(1, 0, 2, 3).reshape(2 * rows, images)
    with jax.named_scope("grad_a"):
        both = dot(gram, norm_a, ((1,), (0,)))
        grad_a = (both[:rows] + both[rows:]) * scale + shifted
    return correlation, grad_a, grad_b


def view_b_columns(view_b, feat, cols_a):
    return lax.dynamic_slice_in_dim(view_b, feat * cols_a, cols_a, 1).astype(f32)


def solution(mesh):
    sizes = (8, 4, 2, 2, 4)
    fine = Mesh(mesh.devices.reshape(sizes), AXES)
    in_specs = (P(DP, FEAT), P(DP, None))
    out_specs = (P(FEAT, DP), P(DP, FEAT), P(None, DP))
    return jax.shard_map(local, mesh=fine, in_specs=in_specs, out_specs=out_specs, check_vma=False)
```

```python
import functools
import jax
import jax.numpy as jnp
from jax import lax
from jax.experimental import pallas as pl
from jax.experimental.pallas import tpu as pltpu
from jax.sharding import Mesh, PartitionSpec as P

epsilon = 1e-05
off_weight = 0.005
f32 = jnp.float32
bf16 = jnp.bfloat16
AXES = ("zl", "y", "c", "zh", "x")
DP = ("zl", "y", "c")
FEAT = ("zh", "x")
SWAP = [(0, 1), (1, 0)]
VMEM_LIMIT = 14 * 1024 * 1024


def exchange(values, axis):
    return lax.all_to_all(values, axis, split_axis=0, concat_axis=0, tiled=False)


def terms(values, count):
    parts = []
    for _ in range(count):
        rounded = lax.reduce_precision(values, 8, 7)
        parts.append(rounded.astype(bf16))
        values = values - rounded
    return parts


def kernel_terms(values, count):
    parts = []
    for _ in range(count):
        parts.append(values.astype(bf16).astype(f32))
        values = values - parts[-1]
    return parts


def dot(left, right, contract):
    return lax.dot_general(left, right, (contract, ((), ())), preferred_element_type=f32)


def statistics(total, square, images):
    mean = total / images
    return mean, lax.rsqrt(square / images - mean * mean + epsilon)


def pack_kernel(ny, nc, idx, a_hbm, b_hbm, send_ref, a_ref, b_ref, sems):
    nz, rows, _ = send_ref.shape
    cols_a = a_ref.shape[1]
    copy_a = pltpu.make_async_copy(a_hbm, a_ref, sems.at[0])
    copy_b = pltpu.make_async_copy(b_hbm, b_ref, sems.at[1])
    copy_b.start()
    copy_a.start()
    copy_a.wait()
    values = a_ref[...]
    for z in range(nz):
        send_ref[z, :, :cols_a] = values
    copy_b.wait()
    lanes = (send_ref.shape[2] - cols_a) // ny
    upper = idx[1] < 2
    column = (idx[1] & 1) * lanes
    keep = (lax.broadcasted_iota(jnp.int32, (rows, lanes), 0) < rows // 2) == upper
    for z in range(nz):
        for y in range(ny):
            pair = []
            for c in range(nc):
                first = ((z * ny + y) * nc + c) * 2 * lanes
                first = pl.multiple_of(first + column, lanes)
                pair.append(b_ref[:, pl.ds(first, lanes)].astype(f32))
            moved = pltpu.roll(jnp.where(upper, pair[1], pair[0]), rows // 2, 0)
            mixed = jnp.where(keep, jnp.where(upper, pair[0], pair[1]), moved)
            send_ref[z, :, cols_a + y * lanes : cols_a + (y + 1) * lanes] = mixed.astype(bf16)


def pack(idx, view_a, view_b, sizes):
    nz, ny, nc, nx = sizes
    rows, cols_a = view_a.shape
    lanes = view_b.shape[1] // (nz * ny * nc * 2)
    return pl.pallas_call(
        functools.partial(pack_kernel, ny, nc),
        out_shape=jax.ShapeDtypeStruct((nz, rows, cols_a + ny * lanes), bf16),
        in_specs=[pl.BlockSpec(memory_space=pltpu.SMEM)] + [pl.BlockSpec(memory_space=pl.ANY)] * 2,
        out_specs=in_vmem(1)[0],
        scratch_shapes=[
            pltpu.VMEM(view_a.shape, bf16),
            pltpu.VMEM(view_b.shape, bf16),
            pltpu.SemaphoreType.DMA((2,)),
        ],
        compiler_params=pltpu.CompilerParams(vmem_limit_bytes=VMEM_LIMIT),
    )(idx, view_a, view_b)


def standardize_kernel(idx, own_ref, other_ref, norm_ref, stat_ref):
    half = own_ref.shape[0]
    cols = norm_ref.shape[1]
    own_place = pl.multiple_of(idx[0] * half, half)
    other_place = pl.multiple_of((1 - idx[0]) * half, half)
    block = 256
    for j in range(cols // block):
        span = slice(j * block, (j + 1) * block)
        own = own_ref[:, span].astype(f32)
        other = other_ref[:, span].astype(f32)
        total = jnp.sum(own, 0, keepdims=True) + jnp.sum(other, 0, keepdims=True)
        square = jnp.sum(own * own, 0, keepdims=True) + jnp.sum(other * other, 0, keepdims=True)
        mean, inverse = statistics(total, square, 2 * half)
        norm_ref[pl.ds(own_place, half), span] = ((own - mean) * inverse).astype(bf16)
        norm_ref[pl.ds(other_place, half), span] = ((other - mean) * inverse).astype(bf16)
        stat_ref[0:1, span] = mean
        stat_ref[1:2, span] = inverse


def in_vmem(count):
    return [pl.BlockSpec(memory_space=pltpu.VMEM)] * count


def standardize_a(idx, own, other, cols):
    half = own.shape[0]
    return pl.pallas_call(
        standardize_kernel,
        out_shape=(
            jax.ShapeDtypeStruct((2 * half, cols), bf16),
            jax.ShapeDtypeStruct((8, cols), f32),
        ),
        in_specs=[pl.BlockSpec(memory_space=pltpu.SMEM)] + in_vmem(2),
        out_specs=in_vmem(2),
        compiler_params=pltpu.CompilerParams(vmem_limit_bytes=VMEM_LIMIT),
        cost_estimate=pl.CostEstimate(
            flops=20 * half * cols, bytes_accessed=8 * half * cols, transcendentals=cols
        ),
    )(idx, own, other)


def tile_kernel(
    nz, ny, nc, nx, idx, a_ref, b_ref, out_ref, part_ref, norm_ref, tail, corr_ref, high, sems
):
    images, cols = norm_ref.shape
    cols_a = a_ref.shape[1]
    part, lanes = b_ref.shape[-2:]
    parts = b_ref.shape[1]
    half = part * parts
    rows = images // (nz * ny * nc)

    deep = part // rows
    keep = lax.broadcasted_iota(jnp.int32, (deep, rows, lanes), 1) < rows // 2
    for h in range(cols // lanes):
        span = slice(h * lanes, (h + 1) * lanes)
        values = [b_ref[c, k, h].astype(f32) for c in range(nc) for k in range(parts)]
        total = sum(jnp.sum(v, 0, keepdims=True) for v in values)
        square = sum(jnp.sum(v * v, 0, keepdims=True) for v in values)
        mean, inverse = statistics(total, square, images)
        values = [((v - mean) * inverse).reshape(deep, rows, lanes) for v in values]
        for c in range(nc):
            first, second = values[2 * c], values[2 * c + 1]
            even = jnp.where(keep, first, pltpu.roll(second, rows // 2, 1))
            odd = jnp.where(keep, pltpu.roll(first, rows // 2, 1), second)
            norm_ref[c * half : (c + 1) * half, span] = jnp.stack([even, odd], 1).reshape(half, lanes).astype(bf16)
        for k, term in enumerate(kernel_terms(mean, 3) + kernel_terms(inverse, 3)):
            tail[8 + k : 9 + k, span] = term
        tail[16:17, span] = inverse

    norm = norm_ref[...]
    ones = jnp.ones((8, cols), bf16)
    copies = []
    for j in range(cols_a // cols):
        span = slice(j * cols, (j + 1) * cols)
        corr = dot(a_ref[:, span], norm, ((0,), (0,))) / images
        corr_ref[span, :] = corr
        place = pl.ds(j * cols, cols)
        copies.append(pltpu.make_async_copy(corr_ref.at[place], out_ref.at[place], sems.at[j]))
        copies[-1].start()
        upper, lower = (v.astype(bf16) for v in kernel_terms(corr * corr, 2))
        sums = dot(ones, upper, ((1,), (1,))) + dot(ones, lower, ((1,), (1,)))
        tail[j : j + 1, :] = sums[0:1]
        high[span, :] = corr.astype(bf16)

    place = pl.multiple_of(idx[2] * cols, cols)
    corr = corr_ref[pl.ds(place, cols), :]
    row = lax.broadcasted_iota(jnp.int32, corr.shape, 0)
    col = lax.broadcasted_iota(jnp.int32, corr.shape, 1)
    diagonal = jnp.sum(jnp.where(row == col, corr, 0.0), 0, keepdims=True)
    for k, part in enumerate(kernel_terms(diagonal, 2)):
        tail[14 + k : 15 + k, :] = part
    shift = -2.0 * (1.0 - diagonal) - 2.0 * off_weight * diagonal
    shift = jnp.where(idx[3] == 1, shift, 0.0)
    chunk = images // nx
    totals = []
    for k in range(nx):
        span = slice(k * chunk, (k + 1) * chunk)
        total = dot(a_ref[span, :], high[...], ((1,), (0,))) * (2.0 * off_weight)
        totals.append(total + a_ref[span, pl.ds(place, cols)].astype(f32) * shift)
    along = 0.0
    for k in range(nx):
        along += jnp.sum(totals[k] * norm_ref[k * chunk : (k + 1) * chunk, :].astype(f32), 0, keepdims=True)
    along = along / images
    for k in range(nx):
        total = totals[k] - norm_ref[k * chunk : (k + 1) * chunk, :].astype(f32) * along
        to = k ^ idx[1]
        to = to ^ (to >> 1)
        part_ref[pl.ds(pl.multiple_of(to * chunk, chunk), chunk), :] = (total * tail[16:17, :]).astype(bf16)
    for copy in copies:
        copy.wait()


def tile(idx, norm_a, parts, sizes):
    nz, ny, nc, nx = sizes
    images, cols_a = norm_a.shape
    cols = parts.shape[2] * parts.shape[4]
    return pl.pallas_call(
        functools.partial(tile_kernel, nz, ny, nc, nx),
        out_shape=(
            jax.ShapeDtypeStruct((cols_a, cols), f32),
            jax.ShapeDtypeStruct((images, cols), bf16),
            jax.ShapeDtypeStruct((images, cols), bf16),
            jax.ShapeDtypeStruct((24, cols), f32),
        ),
        in_specs=[pl.BlockSpec(memory_space=pltpu.SMEM)] + in_vmem(2),
        out_specs=[pl.BlockSpec(memory_space=pl.ANY)] + in_vmem(3),
        scratch_shapes=[
            pltpu.VMEM((cols_a, cols), f32),
            pltpu.VMEM((cols_a, cols), bf16),
            pltpu.SemaphoreType.DMA((cols_a // cols,)),
        ],
        compiler_params=pltpu.CompilerParams(vmem_limit_bytes=VMEM_LIMIT),
        cost_estimate=pl.CostEstimate(
            flops=6 * images * cols_a * cols, bytes_accessed=4 * images * cols_a, transcendentals=0
        ),
    )(idx, norm_a, parts)


def gram_kernel(nz, ny, nc, nx, idx, norm_ref, tail, send_ref):
    images, cols = norm_ref.shape
    rows = images // (nz * ny * nc)
    take = rows // nx
    norm = norm_ref[...]
    picks = nz * ny * nc * take
    out = lax.broadcasted_iota(jnp.int32, (picks, images), 0)
    image = lax.broadcasted_iota(jnp.int32, (picks, images), 1)
    t, c, y, z = out & 1, (out >> 1) & 1, (out >> 2) & 3, out >> 4
    wanted = ((c * ny + y) * nz + z) * rows + idx[1] * take + t
    select = jnp.where(image == wanted, 1.0, 0.0).astype(bf16)
    picked = dot(select, norm, ((1,), (0,))).astype(bf16)
    gram = dot(picked, norm, ((1,), (1,)))
    for z in range(nz):
        send_ref[z, :, :images] = gram[z * 16 : z * 16 + 16].astype(bf16)

    values = tail[0:16, :].astype(bf16)
    for z in range(nz):
        send_ref[z, :, images:] = values


def gram_part(idx, norm_b, tail, sizes):
    nz = sizes[0]
    images, cols = norm_b.shape
    return pl.pallas_call(
        functools.partial(gram_kernel, *sizes),
        out_shape=jax.ShapeDtypeStruct((nz, 16, images + cols), bf16),
        in_specs=[pl.BlockSpec(memory_space=pltpu.SMEM)] + in_vmem(2),
        out_specs=in_vmem(1)[0],
        compiler_params=pltpu.CompilerParams(vmem_limit_bytes=VMEM_LIMIT),
        cost_estimate=pl.CostEstimate(
            flops=8 * images * images * cols, bytes_accessed=16 * images * cols, transcendentals=0
        ),
    )(idx, norm_b, tail)


def local(view_a, view_b):
    nz, ny, nc = (lax.axis_size(a) for a in DP)
    nh, nx = (lax.axis_size(a) for a in FEAT)
    rows, cols_a = view_a.shape
    width = view_b.shape[1]
    cols_b = width // (nz * ny * nc)
    images = rows * nz * ny * nc
    iz, iy, ic = (lax.axis_index(a) for a in DP)
    ih, ix = (lax.axis_index(a) for a in FEAT)
    feat = ih * nx + ix
    n_yc = ny * nc

    with jax.named_scope("gather_z"):
        lanes = cols_b // 2
        idx = jnp.stack([ic, ix, iy * nc + ic, (feat == iz).astype(jnp.int32)]).astype(jnp.int32)
        send = pack(idx, view_a, view_b, (nz, ny, nc, nx))
        got = exchange(send, "zl").reshape(nz * rows, cols_a + ny * lanes)
    with jax.named_scope("gather_y"):
        send = jnp.concatenate(
            [
                jnp.broadcast_to(got[None, :, :cols_a], (ny, nz * rows, cols_a)),
                got[:, cols_a:].reshape(nz * rows, ny, lanes).transpose(1, 0, 2),
            ],
            2,
        )
        got = exchange(send, "y").reshape(ny * nz * rows, cols_a + lanes)
    with jax.named_scope("gather_core_x"):
        got_other = lax.ppermute(got, "c", SWAP)
        half = images // nc
        parts = got[:, cols_a:].reshape(half // rows, nc, rows // nc, lanes).transpose(1, 0, 2, 3)
        parts = parts.reshape(nc, 1, half // nc, lanes)
        parts = jnp.broadcast_to(parts, (nc, nx, half // nc, lanes)).reshape(nc * nx, half // nc, lanes)
        parts = exchange(parts, ("c", "x")).reshape(nc, nx // 2, 2, half // nc, lanes)
    with jax.named_scope("standardize_a"):
        norm_a, stat_a = standardize_a(idx, got, got_other, cols_a)
        norm_a, parts = lax.optimization_barrier((norm_a, parts))
        mean_a, inverse_a = stat_a[0], stat_a[1]
    with jax.named_scope("tile"):
        correlation, part_b, norm_b, tail = tile(idx, norm_a, parts, (nz, ny, nc, nx))

    with jax.named_scope("sum_b_x_reduce_z"):
        n_rows = images // nx
        came = lax.ppermute(part_b[2 * n_rows :], "x", [(i, i ^ 3) for i in range(nx)])
        send = gram_part(idx, norm_b, tail, (nz, ny, nc, nx))
        got = exchange(send, "zl")
        sum_b = part_b[: 2 * n_rows].astype(f32) + came.astype(f32)
        came = lax.ppermute(sum_b[n_rows:].astype(bf16), "x", [(i, i ^ 1) for i in range(nx)])
        sum_b = (sum_b[:n_rows] + came.astype(f32)).astype(bf16)
    with jax.named_scope("reduce_yc"):
        take = rows // nx
        total = jnp.sum(got[:, :, :images].astype(f32), 0).reshape(n_yc, take * images // cols_b, cols_b)
        squares = jnp.sum(got[:, :8, images:].astype(f32), 0)
        aux = lax.dynamic_index_in_dim(got[:, 8:, images:], feat, 0, False).astype(f32)
        aux = jnp.stack([aux[0] + aux[1] + aux[2], aux[3] + aux[4] + aux[5], aux[6] + aux[7], aux[7]])
        right = jnp.concatenate([total, jnp.broadcast_to(aux[None], (n_yc, 4, cols_b))], 1)
        left = jnp.broadcast_to(squares[None], (n_yc, 8, cols_b))
        send = jnp.concatenate([left, right, jnp.zeros((n_yc, 8, 2 * cols_b), f32)], 2)
        other = lax.ppermute(sum_b, "zh", SWAP)
        got = exchange(send, ("y", "c"))[:, :, : 2 * cols_b]
        squares = jnp.sum(got[:, :, :cols_b], 0).reshape(cols_a)
        gram = jnp.sum(got[:, :4, cols_b:], 0)
        mean_f, inverse_f, diag_f = (got[:, 4 + k, cols_b:].reshape(cols_a) for k in range(3))

    with jax.named_scope("shift_a"):
        shift = -2.0 * (1.0 - diag_f) - 2.0 * off_weight * diag_f
        projected = 2.0 * off_weight * squares + shift * diag_f
        own_b = ((view_b_columns(view_b, feat, cols_a) - mean_f) * inverse_f).astype(bf16).astype(f32)
        own_a = ((view_a.astype(f32) - mean_a) * inverse_a).astype(bf16).astype(f32)
        shifted = (own_b * shift - own_a * projected) * inverse_a
        scale = jnp.broadcast_to(2.0 * off_weight / images * inverse_a, (rows, cols_a))
    with jax.named_scope("gather_b_x"):
        sum_b = (sum_b.astype(f32) + other.astype(f32)).astype(bf16)
        upper, lower = terms(gram, 2)
        own = jnp.concatenate([sum_b, upper, lower], 0)
        shifted, scale = lax.optimization_barrier((shifted, scale))
        got = exchange(jnp.broadcast_to(own[None], (nx,) + own.shape), "x")
        grad_b = got[:, :n_rows].reshape(nc, ny, nz, rows, cols_b).transpose(2, 1, 0, 3, 4)
        grad_b = grad_b.reshape(images, cols_b).astype(f32)
        gram = got[:, n_rows:].reshape(nx, 2, take, images).transpose(1, 0, 2, 3).reshape(2 * rows, images)
    with jax.named_scope("grad_a"):
        both = dot(gram, norm_a, ((1,), (0,)))
        grad_a = (both[:rows] + both[rows:]) * scale + shifted
    return correlation, grad_a, grad_b


def view_b_columns(view_b, feat, cols_a):
    return lax.dynamic_slice_in_dim(view_b, feat * cols_a, cols_a, 1).astype(f32)


def solution(mesh):
    sizes = (8, 4, 2, 2, 4)
    fine = Mesh(mesh.devices.reshape(sizes), AXES)
    in_specs = (P(DP, FEAT), P(DP, None))
    out_specs = (P(FEAT, DP), P(DP, FEAT), P(None, DP))
    return jax.shard_map(local, mesh=fine, in_specs=in_specs, out_specs=out_specs, check_vma=False)
```

```python
import functools
import jax
import jax.numpy as jnp
from jax import lax
from jax.experimental import pallas as pl
from jax.experimental.pallas import tpu as pltpu
from jax.sharding import Mesh, PartitionSpec as P

epsilon = 1e-05
off_weight = 0.005
f32 = jnp.float32
bf16 = jnp.bfloat16
AXES = ("zl", "y", "c", "zh", "x")
DP = ("zl", "y", "c")
FEAT = ("zh", "x")
SWAP = [(0, 1), (1, 0)]
VMEM_LIMIT = 14 * 1024 * 1024


def exchange(values, axis):
    return lax.all_to_all(values, axis, split_axis=0, concat_axis=0, tiled=False)


def terms(values, count):
    parts = []
    for _ in range(count):
        rounded = lax.reduce_precision(values, 8, 7)
        parts.append(rounded.astype(bf16))
        values = values - rounded
    return parts


def kernel_terms(values, count):
    parts = []
    for _ in range(count):
        parts.append(values.astype(bf16).astype(f32))
        values = values - parts[-1]
    return parts


def dot(left, right, contract):
    return lax.dot_general(left, right, (contract, ((), ())), preferred_element_type=f32)


def statistics(total, square, images):
    mean = total / images
    return mean, lax.rsqrt(square / images - mean * mean + epsilon)


def pack_kernel(ny, nc, idx, a_hbm, b_hbm, send_ref, a_ref, b_ref, sems):
    nz, rows, _ = send_ref.shape
    cols_a = a_ref.shape[1]
    copy_a = pltpu.make_async_copy(a_hbm, a_ref, sems.at[0])
    copy_b = pltpu.make_async_copy(b_hbm, b_ref, sems.at[1])
    copy_b.start()
    copy_a.start()
    copy_a.wait()
    values = a_ref[...]
    for z in range(nz):
        send_ref[z, :, :cols_a] = values
    copy_b.wait()
    lanes = (send_ref.shape[2] - cols_a) // ny
    upper = idx[1] < 2
    column = (idx[1] & 1) * lanes
    keep = (lax.broadcasted_iota(jnp.int32, (rows, lanes), 0) < rows // 2) == upper
    for z in range(nz):
        for y in range(ny):
            pair = []
            for c in range(nc):
                first = ((z * ny + y) * nc + c) * 2 * lanes
                first = pl.multiple_of(first + column, lanes)
                pair.append(b_ref[:, pl.ds(first, lanes)].astype(f32))
            moved = pltpu.roll(jnp.where(upper, pair[1], pair[0]), rows // 2, 0)
            mixed = jnp.where(keep, jnp.where(upper, pair[0], pair[1]), moved)
            send_ref[z, :, cols_a + y * lanes : cols_a + (y + 1) * lanes] = mixed.astype(bf16)


def pack(idx, view_a, view_b, sizes):
    nz, ny, nc, nx = sizes
    rows, cols_a = view_a.shape
    lanes = view_b.shape[1] // (nz * ny * nc * 2)
    return pl.pallas_call(
        functools.partial(pack_kernel, ny, nc),
        out_shape=jax.ShapeDtypeStruct((nz, rows, cols_a + ny * lanes), bf16),
        in_specs=[pl.BlockSpec(memory_space=pltpu.SMEM)] + [pl.BlockSpec(memory_space=pl.ANY)] * 2,
        out_specs=in_vmem(1)[0],
        scratch_shapes=[
            pltpu.VMEM(view_a.shape, bf16),
            pltpu.VMEM(view_b.shape, bf16),
            pltpu.SemaphoreType.DMA((2,)),
        ],
        compiler_params=pltpu.CompilerParams(vmem_limit_bytes=VMEM_LIMIT),
    )(idx, view_a, view_b)


def standardize_kernel(idx, own_ref, other_ref, norm_ref, stat_ref):
    half = own_ref.shape[0]
    cols = norm_ref.shape[1]
    own_place = pl.multiple_of(idx[0] * half, half)
    other_place = pl.multiple_of((1 - idx[0]) * half, half)
    block = 256
    for j in range(cols // block):
        span = slice(j * block, (j + 1) * block)
        own = own_ref[:, span].astype(f32)
        other = other_ref[:, span].astype(f32)
        total = jnp.sum(own, 0, keepdims=True) + jnp.sum(other, 0, keepdims=True)
        square = jnp.sum(own * own, 0, keepdims=True) + jnp.sum(other * other, 0, keepdims=True)
        mean, inverse = statistics(total, square, 2 * half)
        norm_ref[pl.ds(own_place, half), span] = ((own - mean) * inverse).astype(bf16)
        norm_ref[pl.ds(other_place, half), span] = ((other - mean) * inverse).astype(bf16)
        stat_ref[0:1, span] = mean
        stat_ref[1:2, span] = inverse


def in_vmem(count):
    return [pl.BlockSpec(memory_space=pltpu.VMEM)] * count


def standardize_a(idx, own, other, cols):
    half = own.shape[0]
    return pl.pallas_call(
        standardize_kernel,
        out_shape=(
            jax.ShapeDtypeStruct((2 * half, cols), bf16),
            jax.ShapeDtypeStruct((8, cols), f32),
        ),
        in_specs=[pl.BlockSpec(memory_space=pltpu.SMEM)] + in_vmem(2),
        out_specs=in_vmem(2),
        compiler_params=pltpu.CompilerParams(vmem_limit_bytes=VMEM_LIMIT),
        cost_estimate=pl.CostEstimate(
            flops=20 * half * cols, bytes_accessed=8 * half * cols, transcendentals=cols
        ),
    )(idx, own, other)


def tile_kernel(
    nz, ny, nc, nx, idx, a_ref, b_ref, out_ref, part_ref, norm_ref, tail, corr_ref, high, sems
):
    images, cols = norm_ref.shape
    cols_a = a_ref.shape[1]
    part, lanes = b_ref.shape[-2:]
    parts = b_ref.shape[1]
    half = part * parts
    rows = images // (nz * ny * nc)

    deep = part // rows
    keep = lax.broadcasted_iota(jnp.int32, (deep, rows, lanes), 1) < rows // 2
    for h in range(cols // lanes):
        span = slice(h * lanes, (h + 1) * lanes)
        values = [b_ref[c, k, h].astype(f32) for c in range(nc) for k in range(parts)]
        total = sum(jnp.sum(v, 0, keepdims=True) for v in values)
        square = sum(jnp.sum(v * v, 0, keepdims=True) for v in values)
        mean, inverse = statistics(total, square, images)
        values = [((v - mean) * inverse).reshape(deep, rows, lanes) for v in values]
        for c in range(nc):
            first, second = values[2 * c], values[2 * c + 1]
            even = jnp.where(keep, first, pltpu.roll(second, rows // 2, 1))
            odd = jnp.where(keep, pltpu.roll(first, rows // 2, 1), second)
            norm_ref[c * half : (c + 1) * half, span] = jnp.stack([even, odd], 1).reshape(half, lanes).astype(bf16)
        for k, term in enumerate(kernel_terms(mean, 3) + kernel_terms(inverse, 3)):
            tail[8 + k : 9 + k, span] = term
        tail[16:17, span] = inverse

    norm = norm_ref[...]
    ones = jnp.ones((8, cols), bf16)
    copies = []
    for j in range(cols_a // cols):
        span = slice(j * cols, (j + 1) * cols)
        corr = dot(a_ref[:, span], norm, ((0,), (0,))) / images
        corr_ref[span, :] = corr
        place = pl.ds(j * cols, cols)
        copies.append(pltpu.make_async_copy(corr_ref.at[place], out_ref.at[place], sems.at[j]))
        copies[-1].start()
        upper, lower = (v.astype(bf16) for v in kernel_terms(corr * corr, 2))
        sums = dot(ones, upper, ((1,), (1,))) + dot(ones, lower, ((1,), (1,)))
        tail[j : j + 1, :] = sums[0:1]
        high[span, :] = corr.astype(bf16)

    place = pl.multiple_of(idx[2] * cols, cols)
    corr = corr_ref[pl.ds(place, cols), :]
    row = lax.broadcasted_iota(jnp.int32, corr.shape, 0)
    col = lax.broadcasted_iota(jnp.int32, corr.shape, 1)
    diagonal = jnp.sum(jnp.where(row == col, corr, 0.0), 0, keepdims=True)
    for k, part in enumerate(kernel_terms(diagonal, 2)):
        tail[14 + k : 15 + k, :] = part
    shift = -2.0 * (1.0 - diagonal) - 2.0 * off_weight * diagonal
    shift = jnp.where(idx[3] == 1, shift, 0.0)
    chunk = images // nx
    totals = []
    for k in range(nx):
        span = slice(k * chunk, (k + 1) * chunk)
        total = dot(a_ref[span, :], high[...], ((1,), (0,))) * (2.0 * off_weight)
        totals.append(total + a_ref[span, pl.ds(place, cols)].astype(f32) * shift)
    along = 0.0
    for k in range(nx):
        along += jnp.sum(totals[k] * norm_ref[k * chunk : (k + 1) * chunk, :].astype(f32), 0, keepdims=True)
    along = along / images
    for k in range(nx):
        total = totals[k] - norm_ref[k * chunk : (k + 1) * chunk, :].astype(f32) * along
        to = k ^ idx[1]
        to = to ^ (to >> 1)
        part_ref[pl.ds(pl.multiple_of(to * chunk, chunk), chunk), :] = (total * tail[16:17, :]).astype(bf16)
    for copy in copies:
        copy.wait()


def tile(idx, norm_a, parts, sizes):
    nz, ny, nc, nx = sizes
    images, cols_a = norm_a.shape
    cols = parts.shape[2] * parts.shape[4]
    return pl.pallas_call(
        functools.partial(tile_kernel, nz, ny, nc, nx),
        out_shape=(
            jax.ShapeDtypeStruct((cols_a, cols), f32),
            jax.ShapeDtypeStruct((images, cols), bf16),
            jax.ShapeDtypeStruct((images, cols), bf16),
            jax.ShapeDtypeStruct((24, cols), f32),
        ),
        in_specs=[pl.BlockSpec(memory_space=pltpu.SMEM)] + in_vmem(2),
        out_specs=[pl.BlockSpec(memory_space=pl.ANY)] + in_vmem(3),
        scratch_shapes=[
            pltpu.VMEM((cols_a, cols), f32),
            pltpu.VMEM((cols_a, cols), bf16),
            pltpu.SemaphoreType.DMA((cols_a // cols,)),
        ],
        compiler_params=pltpu.CompilerParams(vmem_limit_bytes=VMEM_LIMIT),
        cost_estimate=pl.CostEstimate(
            flops=6 * images * cols_a * cols, bytes_accessed=4 * images * cols_a, transcendentals=0
        ),
    )(idx, norm_a, parts)


def gram_kernel(nz, ny, nc, nx, idx, norm_ref, tail, send_ref):
    images, cols = norm_ref.shape
    rows = images // (nz * ny * nc)
    take = rows // nx
    norm = norm_ref[...]
    picks = nz * ny * nc * take
    out = lax.broadcasted_iota(jnp.int32, (picks, images), 0)
    image = lax.broadcasted_iota(jnp.int32, (picks, images), 1)
    t, c, y, z = out & 1, (out >> 1) & 1, (out >> 2) & 3, out >> 4
    wanted = ((c * ny + y) * nz + z) * rows + idx[1] * take + t
    select = jnp.where(image == wanted, 1.0, 0.0).astype(bf16)
    picked = dot(select, norm, ((1,), (0,))).astype(bf16)
    gram = dot(picked, norm, ((1,), (1,)))
    for z in range(nz):
        send_ref[z, :, :images] = gram[z * 16 : z * 16 + 16].astype(bf16)

    values = tail[0:16, :].astype(bf16)
    for z in range(nz):
        send_ref[z, :, images:] = values


def gram_part(idx, norm_b, tail, sizes):
    nz = sizes[0]
    images, cols = norm_b.shape
    return pl.pallas_call(
        functools.partial(gram_kernel, *sizes),
        out_shape=jax.ShapeDtypeStruct((nz, 16, images + cols), bf16),
        in_specs=[pl.BlockSpec(memory_space=pltpu.SMEM)] + in_vmem(2),
        out_specs=in_vmem(1)[0],
        compiler_params=pltpu.CompilerParams(vmem_limit_bytes=VMEM_LIMIT),
        cost_estimate=pl.CostEstimate(
            flops=8 * images * images * cols, bytes_accessed=16 * images * cols, transcendentals=0
        ),
    )(idx, norm_b, tail)


def finish_kernel(nz, ny, nc, got_ref, norm_ref, shifted_ref, scale_ref, grad_a_ref, grad_b_ref, gram):
    nx, rows_x, cols = got_ref.shape
    images = norm_ref.shape[0]
    rows = shifted_ref.shape[0]
    n_rows = images // nx
    wide = images // cols
    take = rows // nx
    for x in range(nx):
        values = got_ref[x, n_rows:, :].astype(f32)
        for part in range(2):
            for t in range(take):
                for w in range(wide):
                    line = (part * take + t) * wide + w
                    to = part * rows + x * take + t
                    gram[to : to + 1, w * cols : (w + 1) * cols] = values[line : line + 1]
    both = dot(gram[...].astype(bf16), norm_ref[...], ((1,), (0,)))
    grad_a_ref[...] = (both[:rows] + both[rows:]) * scale_ref[...] + shifted_ref[...]
    for x in range(nx):
        values = got_ref[x, :n_rows, :].astype(f32)
        for k in range(n_rows // rows):
            block = x * (n_rows // rows) + k
            c, y, z = block // (ny * nz), block // nz % ny, block % nz
            to = ((z * ny + y) * nc + c) * rows
            grad_b_ref[to : to + rows, :] = values[k * rows : (k + 1) * rows]


def finish(got, norm_a, shifted, scale, sizes):
    images, cols_a = norm_a.shape
    rows, cols = shifted.shape[0], got.shape[2]
    return pl.pallas_call(
        functools.partial(finish_kernel, *sizes[:3]),
        out_shape=(
            jax.ShapeDtypeStruct((rows, cols_a), f32),
            jax.ShapeDtypeStruct((images, cols), f32),
        ),
        in_specs=in_vmem(4),
        out_specs=in_vmem(2),
        scratch_shapes=[pltpu.VMEM((2 * rows, images), f32)],
        compiler_params=pltpu.CompilerParams(vmem_limit_bytes=VMEM_LIMIT),
    )(got, norm_a, shifted, scale)


def local(view_a, view_b):
    nz, ny, nc = (lax.axis_size(a) for a in DP)
    nh, nx = (lax.axis_size(a) for a in FEAT)
    rows, cols_a = view_a.shape
    width = view_b.shape[1]
    cols_b = width // (nz * ny * nc)
    images = rows * nz * ny * nc
    iz, iy, ic = (lax.axis_index(a) for a in DP)
    ih, ix = (lax.axis_index(a) for a in FEAT)
    feat = ih * nx + ix
    n_yc = ny * nc

    with jax.named_scope("gather_z"):
        lanes = cols_b // 2
        idx = jnp.stack([ic, ix, iy * nc + ic, (feat == iz).astype(jnp.int32)]).astype(jnp.int32)
        send = pack(idx, view_a, view_b, (nz, ny, nc, nx))
        got = exchange(send, "zl").reshape(nz * rows, cols_a + ny * lanes)
    with jax.named_scope("gather_y"):
        send = jnp.concatenate(
            [
                jnp.broadcast_to(got[None, :, :cols_a], (ny, nz * rows, cols_a)),
                got[:, cols_a:].reshape(nz * rows, ny, lanes).transpose(1, 0, 2),
            ],
            2,
        )
        got = exchange(send, "y").reshape(ny * nz * rows, cols_a + lanes)
    with jax.named_scope("gather_core_x"):
        got_other = lax.ppermute(got, "c", SWAP)
        half = images // nc
        parts = got[:, cols_a:].reshape(half // rows, nc, rows // nc, lanes).transpose(1, 0, 2, 3)
        parts = parts.reshape(nc, 1, half // nc, lanes)
        parts = jnp.broadcast_to(parts, (nc, nx, half // nc, lanes)).reshape(nc * nx, half // nc, lanes)
        parts = exchange(parts, ("c", "x")).reshape(nc, nx // 2, 2, half // nc, lanes)
    with jax.named_scope("standardize_a"):
        norm_a, stat_a = standardize_a(idx, got, got_other, cols_a)
        norm_a, parts = lax.optimization_barrier((norm_a, parts))
        mean_a, inverse_a = stat_a[0], stat_a[1]
    with jax.named_scope("tile"):
        correlation, part_b, norm_b, tail = tile(idx, norm_a, parts, (nz, ny, nc, nx))

    with jax.named_scope("sum_b_x_reduce_z"):
        n_rows = images // nx
        came = lax.ppermute(part_b[2 * n_rows :], "x", [(i, i ^ 3) for i in range(nx)])
        send = gram_part(idx, norm_b, tail, (nz, ny, nc, nx))
        got = exchange(send, "zl")
        sum_b = part_b[: 2 * n_rows].astype(f32) + came.astype(f32)
        came = lax.ppermute(sum_b[n_rows:].astype(bf16), "x", [(i, i ^ 1) for i in range(nx)])
        sum_b = (sum_b[:n_rows] + came.astype(f32)).astype(bf16)
    with jax.named_scope("reduce_yc"):
        take = rows // nx
        total = jnp.sum(got[:, :, :images].astype(f32), 0).reshape(n_yc, take * images // cols_b, cols_b)
        squares = jnp.sum(got[:, :8, images:].astype(f32), 0)
        aux = lax.dynamic_index_in_dim(got[:, 8:, images:], feat, 0, False).astype(f32)
        aux = jnp.stack([aux[0] + aux[1] + aux[2], aux[3] + aux[4] + aux[5], aux[6] + aux[7], aux[7]])
        right = jnp.concatenate([total, jnp.broadcast_to(aux[None], (n_yc, 4, cols_b))], 1)
        left = jnp.broadcast_to(squares[None], (n_yc, 8, cols_b))
        send = jnp.concatenate([left, right, jnp.zeros((n_yc, 8, 2 * cols_b), f32)], 2)
        other = lax.ppermute(sum_b, "zh", SWAP)
        got = exchange(send, ("y", "c"))[:, :, : 2 * cols_b]
        squares = jnp.sum(got[:, :, :cols_b], 0).reshape(cols_a)
        gram = jnp.sum(got[:, :4, cols_b:], 0)
        mean_f, inverse_f, diag_f = (got[:, 4 + k, cols_b:].reshape(cols_a) for k in range(3))

    with jax.named_scope("shift_a"):
        shift = -2.0 * (1.0 - diag_f) - 2.0 * off_weight * diag_f
        projected = 2.0 * off_weight * squares + shift * diag_f
        own_b = ((view_b_columns(view_b, feat, cols_a) - mean_f) * inverse_f).astype(bf16).astype(f32)
        own_a = ((view_a.astype(f32) - mean_a) * inverse_a).astype(bf16).astype(f32)
        shifted = (own_b * shift - own_a * projected) * inverse_a
        scale = jnp.broadcast_to(2.0 * off_weight / images * inverse_a, (rows, cols_a))
    with jax.named_scope("gather_b_x"):
        sum_b = (sum_b.astype(f32) + other.astype(f32)).astype(bf16)
        upper, lower = terms(gram, 2)
        own = jnp.concatenate([sum_b, upper, lower], 0)
        shifted, scale = lax.optimization_barrier((shifted, scale))
        got = exchange(jnp.broadcast_to(own[None], (nx,) + own.shape), "x")
    with jax.named_scope("finish"):
        grad_a, grad_b = finish(got, norm_a, shifted, scale, (nz, ny, nc, nx))
    return correlation, grad_a, grad_b


def view_b_columns(view_b, feat, cols_a):
    return lax.dynamic_slice_in_dim(view_b, feat * cols_a, cols_a, 1).astype(f32)


def solution(mesh):
    sizes = (8, 4, 2, 2, 4)
    fine = Mesh(mesh.devices.reshape(sizes), AXES)
    in_specs = (P(DP, FEAT), P(DP, None))
    out_specs = (P(FEAT, DP), P(DP, FEAT), P(None, DP))
    return jax.shard_map(local, mesh=fine, in_specs=in_specs, out_specs=out_specs, check_vma=False)
```

```python
import functools
import jax
import jax.numpy as jnp
from jax import lax
from jax.experimental import pallas as pl
from jax.experimental.pallas import tpu as pltpu
from jax.sharding import Mesh, PartitionSpec as P

epsilon = 1e-05
off_weight = 0.005
f32 = jnp.float32
bf16 = jnp.bfloat16
AXES = ("zl", "y", "c", "zh", "x")
DP = ("zl", "y", "c")
FEAT = ("zh", "x")
SWAP = [(0, 1), (1, 0)]
VMEM_LIMIT = 14 * 1024 * 1024


def exchange(values, axis):
    return lax.all_to_all(values, axis, split_axis=0, concat_axis=0, tiled=False)


def terms(values, count):
    parts = []
    for _ in range(count):
        rounded = lax.reduce_precision(values, 8, 7)
        parts.append(rounded.astype(bf16))
        values = values - rounded
    return parts


def kernel_terms(values, count):
    parts = []
    for _ in range(count):
        parts.append(values.astype(bf16).astype(f32))
        values = values - parts[-1]
    return parts


def dot(left, right, contract):
    return lax.dot_general(left, right, (contract, ((), ())), preferred_element_type=f32)


def statistics(total, square, images):
    mean = total / images
    return mean, lax.rsqrt(square / images - mean * mean + epsilon)


def standardize_kernel(idx, own_ref, other_ref, norm_ref, stat_ref):
    half = own_ref.shape[0]
    cols = norm_ref.shape[1]
    own_place = pl.multiple_of(idx[0] * half, half)
    other_place = pl.multiple_of((1 - idx[0]) * half, half)
    block = 256
    for j in range(cols // block):
        span = slice(j * block, (j + 1) * block)
        own = own_ref[:, span].astype(f32)
        other = other_ref[:, span].astype(f32)
        total = jnp.sum(own, 0, keepdims=True) + jnp.sum(other, 0, keepdims=True)
        square = jnp.sum(own * own, 0, keepdims=True) + jnp.sum(other * other, 0, keepdims=True)
        mean, inverse = statistics(total, square, 2 * half)
        norm_ref[pl.ds(own_place, half), span] = ((own - mean) * inverse).astype(bf16)
        norm_ref[pl.ds(other_place, half), span] = ((other - mean) * inverse).astype(bf16)
        stat_ref[0:1, span] = mean
        stat_ref[1:2, span] = inverse


def in_vmem(count):
    return [pl.BlockSpec(memory_space=pltpu.VMEM)] * count


def standardize_a(idx, own, other, cols):
    half = own.shape[0]
    return pl.pallas_call(
        standardize_kernel,
        out_shape=(
            jax.ShapeDtypeStruct((2 * half, cols), bf16),
            jax.ShapeDtypeStruct((8, cols), f32),
        ),
        in_specs=[pl.BlockSpec(memory_space=pltpu.SMEM)] + in_vmem(2),
        out_specs=in_vmem(2),
        compiler_params=pltpu.CompilerParams(vmem_limit_bytes=VMEM_LIMIT),
        cost_estimate=pl.CostEstimate(
            flops=20 * half * cols, bytes_accessed=8 * half * cols, transcendentals=cols
        ),
    )(idx, own, other)


def tile_kernel(
    nz, ny, nc, nx, idx, a_ref, b_ref, out_ref, part_ref, norm_ref, tail, corr_ref, high, sems
):
    images, cols = norm_ref.shape
    cols_a = a_ref.shape[1]
    part, lanes = b_ref.shape[-2:]
    parts = b_ref.shape[1]
    half = part * parts
    rows = images // (nz * ny * nc)

    deep = part // rows
    keep = lax.broadcasted_iota(jnp.int32, (deep, rows, lanes), 1) < rows // 2
    for h in range(cols // lanes):
        span = slice(h * lanes, (h + 1) * lanes)
        values = [b_ref[c, k, h].astype(f32) for c in range(nc) for k in range(parts)]
        total = sum(jnp.sum(v, 0, keepdims=True) for v in values)
        square = sum(jnp.sum(v * v, 0, keepdims=True) for v in values)
        mean, inverse = statistics(total, square, images)
        values = [((v - mean) * inverse).reshape(deep, rows, lanes) for v in values]
        for c in range(nc):
            first, second = values[2 * c], values[2 * c + 1]
            even = jnp.where(keep, first, pltpu.roll(second, rows // 2, 1))
            odd = jnp.where(keep, pltpu.roll(first, rows // 2, 1), second)
            norm_ref[c * half : (c + 1) * half, span] = jnp.stack([even, odd], 1).reshape(half, lanes).astype(bf16)
        for k, term in enumerate(kernel_terms(mean, 3) + kernel_terms(inverse, 3)):
            tail[8 + k : 9 + k, span] = term
        tail[16:17, span] = inverse

    norm = norm_ref[...]
    ones = jnp.ones((8, cols), bf16)
    copies = []
    for j in range(cols_a // cols):
        span = slice(j * cols, (j + 1) * cols)
        corr = dot(a_ref[:, span], norm, ((0,), (0,))) / images
        corr_ref[span, :] = corr
        place = pl.ds(j * cols, cols)
        copies.append(pltpu.make_async_copy(corr_ref.at[place], out_ref.at[place], sems.at[j]))
        copies[-1].start()
        upper, lower = (v.astype(bf16) for v in kernel_terms(corr * corr, 2))
        sums = dot(ones, upper, ((1,), (1,))) + dot(ones, lower, ((1,), (1,)))
        tail[j : j + 1, :] = sums[0:1]
        high[span, :] = corr.astype(bf16)

    place = pl.multiple_of(idx[2] * cols, cols)
    corr = corr_ref[pl.ds(place, cols), :]
    row = lax.broadcasted_iota(jnp.int32, corr.shape, 0)
    col = lax.broadcasted_iota(jnp.int32, corr.shape, 1)
    diagonal = jnp.sum(jnp.where(row == col, corr, 0.0), 0, keepdims=True)
    for k, part in enumerate(kernel_terms(diagonal, 2)):
        tail[14 + k : 15 + k, :] = part
    shift = -2.0 * (1.0 - diagonal) - 2.0 * off_weight * diagonal
    shift = jnp.where(idx[3] == 1, shift, 0.0)
    chunk = images // nx
    totals = []
    for k in range(nx):
        span = slice(k * chunk, (k + 1) * chunk)
        total = dot(a_ref[span, :], high[...], ((1,), (0,))) * (2.0 * off_weight)
        totals.append(total + a_ref[span, pl.ds(place, cols)].astype(f32) * shift)
    along = 0.0
    for k in range(nx):
        along += jnp.sum(totals[k] * norm_ref[k * chunk : (k + 1) * chunk, :].astype(f32), 0, keepdims=True)
    along = along / images
    for k in range(nx):
        total = totals[k] - norm_ref[k * chunk : (k + 1) * chunk, :].astype(f32) * along
        to = k ^ idx[1]
        to = to ^ (to >> 1)
        part_ref[pl.ds(pl.multiple_of(to * chunk, chunk), chunk), :] = (total * tail[16:17, :]).astype(bf16)
    for copy in copies:
        copy.wait()


def tile(idx, norm_a, parts, sizes):
    nz, ny, nc, nx = sizes
    images, cols_a = norm_a.shape
    cols = parts.shape[2] * parts.shape[4]
    return pl.pallas_call(
        functools.partial(tile_kernel, nz, ny, nc, nx),
        out_shape=(
            jax.ShapeDtypeStruct((cols_a, cols), f32),
            jax.ShapeDtypeStruct((images, cols), bf16),
            jax.ShapeDtypeStruct((images, cols), bf16),
            jax.ShapeDtypeStruct((24, cols), f32),
        ),
        in_specs=[pl.BlockSpec(memory_space=pltpu.SMEM)] + in_vmem(2),
        out_specs=[pl.BlockSpec(memory_space=pl.ANY)] + in_vmem(3),
        scratch_shapes=[
            pltpu.VMEM((cols_a, cols), f32),
            pltpu.VMEM((cols_a, cols), bf16),
            pltpu.SemaphoreType.DMA((cols_a // cols,)),
        ],
        compiler_params=pltpu.CompilerParams(vmem_limit_bytes=VMEM_LIMIT),
        cost_estimate=pl.CostEstimate(
            flops=6 * images * cols_a * cols, bytes_accessed=4 * images * cols_a, transcendentals=0
        ),
    )(idx, norm_a, parts)


def gram_kernel(nz, ny, nc, nx, idx, norm_ref, tail, send_ref):
    images, cols = norm_ref.shape
    rows = images // (nz * ny * nc)
    take = rows // nx
    norm = norm_ref[...]
    picks = nz * ny * nc * take
    out = lax.broadcasted_iota(jnp.int32, (picks, images), 0)
    image = lax.broadcasted_iota(jnp.int32, (picks, images), 1)
    t, c, y, z = out & 1, (out >> 1) & 1, (out >> 2) & 3, out >> 4
    wanted = ((c * ny + y) * nz + z) * rows + idx[1] * take + t
    select = jnp.where(image == wanted, 1.0, 0.0).astype(bf16)
    picked = dot(select, norm, ((1,), (0,))).astype(bf16)
    gram = dot(picked, norm, ((1,), (1,)))
    for z in range(nz):
        send_ref[z, :, :images] = gram[z * 16 : z * 16 + 16].astype(bf16)

    values = tail[0:16, :].astype(bf16)
    for z in range(nz):
        send_ref[z, :, images:] = values


def gram_part(idx, norm_b, tail, sizes):
    nz = sizes[0]
    images, cols = norm_b.shape
    return pl.pallas_call(
        functools.partial(gram_kernel, *sizes),
        out_shape=jax.ShapeDtypeStruct((nz, 16, images + cols), bf16),
        in_specs=[pl.BlockSpec(memory_space=pltpu.SMEM)] + in_vmem(2),
        out_specs=in_vmem(1)[0],
        compiler_params=pltpu.CompilerParams(vmem_limit_bytes=VMEM_LIMIT),
        cost_estimate=pl.CostEstimate(
            flops=8 * images * images * cols, bytes_accessed=16 * images * cols, transcendentals=0
        ),
    )(idx, norm_b, tail)


def finish_kernel(nz, ny, nc, got_ref, norm_ref, shifted_ref, scale_ref, grad_a_ref, grad_b_ref, gram):
    nx, rows_x, cols = got_ref.shape
    images = norm_ref.shape[0]
    rows = shifted_ref.shape[0]
    n_rows = images // nx
    wide = images // cols
    take = rows // nx
    for x in range(nx):
        values = got_ref[x, n_rows:, :].astype(f32)
        for part in range(2):
            for t in range(take):
                for w in range(wide):
                    line = (part * take + t) * wide + w
                    to = part * rows + x * take + t
                    gram[to : to + 1, w * cols : (w + 1) * cols] = values[line : line + 1]
    both = dot(gram[...].astype(bf16), norm_ref[...], ((1,), (0,)))
    grad_a_ref[...] = (both[:rows] + both[rows:]) * scale_ref[...] + shifted_ref[...]
    for x in range(nx):
        values = got_ref[x, :n_rows, :].astype(f32)
        for k in range(n_rows // rows):
            block = x * (n_rows // rows) + k
            c, y, z = block // (ny * nz), block // nz % ny, block % nz
            to = ((z * ny + y) * nc + c) * rows
            grad_b_ref[to : to + rows, :] = values[k * rows : (k + 1) * rows]


def finish(got, norm_a, shifted, scale, sizes):
    images, cols_a = norm_a.shape
    rows, cols = shifted.shape[0], got.shape[2]
    return pl.pallas_call(
        functools.partial(finish_kernel, *sizes[:3]),
        out_shape=(
            jax.ShapeDtypeStruct((rows, cols_a), f32),
            jax.ShapeDtypeStruct((images, cols), f32),
        ),
        in_specs=in_vmem(4),
        out_specs=in_vmem(2),
        scratch_shapes=[pltpu.VMEM((2 * rows, images), f32)],
        compiler_params=pltpu.CompilerParams(vmem_limit_bytes=VMEM_LIMIT),
    )(got, norm_a, shifted, scale)


def local(view_a, view_b):
    nz, ny, nc = (lax.axis_size(a) for a in DP)
    nh, nx = (lax.axis_size(a) for a in FEAT)
    rows, cols_a = view_a.shape
    width = view_b.shape[1]
    cols_b = width // (nz * ny * nc)
    images = rows * nz * ny * nc
    iz, iy, ic = (lax.axis_index(a) for a in DP)
    ih, ix = (lax.axis_index(a) for a in FEAT)
    feat = ih * nx + ix
    n_yc = ny * nc

    with jax.named_scope("gather_z"):
        lanes = cols_b // 2
        idx = jnp.stack([ic, ix, iy * nc + ic, (feat == iz).astype(jnp.int32)]).astype(jnp.int32)
        quarter = view_b.reshape(2, rows // 2, nz * ny, nc, 2, lanes)
        quarter = lax.dynamic_index_in_dim(quarter, ix // 2, 0, False)
        quarter = lax.dynamic_index_in_dim(quarter, ix % 2, 3, False)
        quarter = quarter.transpose(2, 0, 1, 3).reshape(rows, nz, ny * lanes).transpose(1, 0, 2)
        send = jnp.concatenate([jnp.broadcast_to(view_a[None], (nz, rows, cols_a)), quarter], 2)
        got = exchange(send, "zl").reshape(nz * rows, cols_a + ny * lanes)
    with jax.named_scope("gather_y"):
        send = jnp.concatenate(
            [
                jnp.broadcast_to(got[None, :, :cols_a], (ny, nz * rows, cols_a)),
                got[:, cols_a:].reshape(nz * rows, ny, lanes).transpose(1, 0, 2),
            ],
            2,
        )
        got = exchange(send, "y").reshape(ny * nz * rows, cols_a + lanes)
    with jax.named_scope("gather_core_x"):
        got_other = lax.ppermute(got, "c", SWAP)
        half = images // nc
        parts = got[:, cols_a:].reshape(half // rows, nc, rows // nc, lanes).transpose(1, 0, 2, 3)
        parts = parts.reshape(nc, 1, half // nc, lanes)
        parts = jnp.broadcast_to(parts, (nc, nx, half // nc, lanes)).reshape(nc * nx, half // nc, lanes)
        parts = exchange(parts, ("c", "x")).reshape(nc, nx // 2, 2, half // nc, lanes)
    with jax.named_scope("standardize_a"):
        norm_a, stat_a = standardize_a(idx, got, got_other, cols_a)
        norm_a, parts = lax.optimization_barrier((norm_a, parts))
        mean_a, inverse_a = stat_a[0], stat_a[1]
    with jax.named_scope("tile"):
        correlation, part_b, norm_b, tail = tile(idx, norm_a, parts, (nz, ny, nc, nx))

    with jax.named_scope("sum_b_x_reduce_z"):
        n_rows = images // nx
        came = lax.ppermute(part_b[2 * n_rows :], "x", [(i, i ^ 3) for i in range(nx)])
        send = gram_part(idx, norm_b, tail, (nz, ny, nc, nx))
        got = exchange(send, "zl")
        sum_b = part_b[: 2 * n_rows].astype(f32) + came.astype(f32)
        came = lax.ppermute(sum_b[n_rows:].astype(bf16), "x", [(i, i ^ 1) for i in range(nx)])
        sum_b = (sum_b[:n_rows] + came.astype(f32)).astype(bf16)
    with jax.named_scope("reduce_yc"):
        take = rows // nx
        total = jnp.sum(got[:, :, :images].astype(f32), 0).reshape(n_yc, take * images // cols_b, cols_b)
        squares = jnp.sum(got[:, :8, images:].astype(f32), 0)
        aux = lax.dynamic_index_in_dim(got[:, 8:, images:], feat, 0, False).astype(f32)
        aux = jnp.stack([aux[0] + aux[1] + aux[2], aux[3] + aux[4] + aux[5], aux[6] + aux[7], aux[7]])
        right = jnp.concatenate([total, jnp.broadcast_to(aux[None], (n_yc, 4, cols_b))], 1)
        left = jnp.broadcast_to(squares[None], (n_yc, 8, cols_b))
        send = jnp.concatenate([left, right, jnp.zeros((n_yc, 8, 2 * cols_b), f32)], 2)
        other = lax.ppermute(sum_b, "zh", SWAP)
        got = exchange(send, ("y", "c"))[:, :, : 2 * cols_b]
        squares = jnp.sum(got[:, :, :cols_b], 0).reshape(cols_a)
        gram = jnp.sum(got[:, :4, cols_b:], 0)
        mean_f, inverse_f, diag_f = (got[:, 4 + k, cols_b:].reshape(cols_a) for k in range(3))

    with jax.named_scope("shift_a"):
        shift = -2.0 * (1.0 - diag_f) - 2.0 * off_weight * diag_f
        projected = 2.0 * off_weight * squares + shift * diag_f
        own_b = ((view_b_columns(view_b, feat, cols_a) - mean_f) * inverse_f).astype(bf16).astype(f32)
        own_a = ((view_a.astype(f32) - mean_a) * inverse_a).astype(bf16).astype(f32)
        shifted = (own_b * shift - own_a * projected) * inverse_a
        scale = jnp.broadcast_to(2.0 * off_weight / images * inverse_a, (rows, cols_a))
    with jax.named_scope("gather_b_x"):
        sum_b = (sum_b.astype(f32) + other.astype(f32)).astype(bf16)
        upper, lower = terms(gram, 2)
        own = jnp.concatenate([sum_b, upper, lower, jnp.zeros((8, cols_b), bf16)], 0)
        shifted, scale = lax.optimization_barrier((shifted, scale))
        got = exchange(jnp.broadcast_to(own[None], (nx,) + own.shape), "x")
    with jax.named_scope("finish"):
        grad_a, grad_b = finish(got, norm_a, shifted, scale, (nz, ny, nc, nx))
    return correlation, grad_a, grad_b


def view_b_columns(view_b, feat, cols_a):
    return lax.dynamic_slice_in_dim(view_b, feat * cols_a, cols_a, 1).astype(f32)


def solution(mesh):
    sizes = (8, 4, 2, 2, 4)
    fine = Mesh(mesh.devices.reshape(sizes), AXES)
    in_specs = (P(DP, FEAT), P(DP, None))
    out_specs = (P(FEAT, DP), P(DP, FEAT), P(None, DP))
    return jax.shard_map(local, mesh=fine, in_specs=in_specs, out_specs=out_specs, check_vma=False)
```

```python
import functools
import jax
import jax.numpy as jnp
from jax import lax
from jax.experimental import pallas as pl
from jax.experimental.pallas import tpu as pltpu
from jax.sharding import Mesh, PartitionSpec as P

epsilon = 1e-05
off_weight = 0.005
f32 = jnp.float32
bf16 = jnp.bfloat16
AXES = ("zl", "y", "c", "zh", "x")
DP = ("zl", "y", "c")
FEAT = ("zh", "x")
SWAP = [(0, 1), (1, 0)]
VMEM_LIMIT = 14 * 1024 * 1024


def exchange(values, axis):
    return lax.all_to_all(values, axis, split_axis=0, concat_axis=0, tiled=False)


def terms(values, count):
    parts = []
    for _ in range(count):
        rounded = lax.reduce_precision(values, 8, 7)
        parts.append(rounded.astype(bf16))
        values = values - rounded
    return parts


def kernel_terms(values, count):
    parts = []
    for _ in range(count):
        parts.append(values.astype(bf16).astype(f32))
        values = values - parts[-1]
    return parts


def dot(left, right, contract):
    return lax.dot_general(left, right, (contract, ((), ())), preferred_element_type=f32)


def statistics(total, square, images):
    mean = total / images
    return mean, lax.rsqrt(square / images - mean * mean + epsilon)


def standardize_kernel(idx, own_ref, other_ref, norm_ref, stat_ref):
    half = own_ref.shape[0]
    cols = norm_ref.shape[1]
    own_place = pl.multiple_of(idx[0] * half, half)
    other_place = pl.multiple_of((1 - idx[0]) * half, half)
    block = 256
    for j in range(cols // block):
        span = slice(j * block, (j + 1) * block)
        own = own_ref[:, span].astype(f32)
        other = other_ref[:, span].astype(f32)
        total = jnp.sum(own, 0, keepdims=True) + jnp.sum(other, 0, keepdims=True)
        square = jnp.sum(own * own, 0, keepdims=True) + jnp.sum(other * other, 0, keepdims=True)
        mean, inverse = statistics(total, square, 2 * half)
        norm_ref[pl.ds(own_place, half), span] = ((own - mean) * inverse).astype(bf16)
        norm_ref[pl.ds(other_place, half), span] = ((other - mean) * inverse).astype(bf16)
        stat_ref[0:1, span] = mean
        stat_ref[1:2, span] = inverse


def in_vmem(count):
    return [pl.BlockSpec(memory_space=pltpu.VMEM)] * count


def standardize_a(idx, own, other, cols):
    half = own.shape[0]
    return pl.pallas_call(
        standardize_kernel,
        out_shape=(
            jax.ShapeDtypeStruct((2 * half, cols), bf16),
            jax.ShapeDtypeStruct((8, cols), f32),
        ),
        in_specs=[pl.BlockSpec(memory_space=pltpu.SMEM)] + in_vmem(2),
        out_specs=in_vmem(2),
        compiler_params=pltpu.CompilerParams(vmem_limit_bytes=VMEM_LIMIT),
        cost_estimate=pl.CostEstimate(
            flops=20 * half * cols, bytes_accessed=8 * half * cols, transcendentals=cols
        ),
    )(idx, own, other)


def tile_kernel(
    nz, ny, nc, nx, idx, a_ref, b_ref, out_ref, part_ref, norm_ref, tail, corr_ref, high, sems
):
    images, cols = norm_ref.shape
    cols_a = a_ref.shape[1]
    part, lanes = b_ref.shape[-2:]
    parts = b_ref.shape[1]
    half = part * parts
    rows = images // (nz * ny * nc)

    deep = part // rows
    keep = lax.broadcasted_iota(jnp.int32, (deep, rows, lanes), 1) < rows // 2
    for h in range(cols // lanes):
        span = slice(h * lanes, (h + 1) * lanes)
        values = [b_ref[c, k, h].astype(f32) for c in range(nc) for k in range(parts)]
        total = sum(jnp.sum(v, 0, keepdims=True) for v in values)
        square = sum(jnp.sum(v * v, 0, keepdims=True) for v in values)
        mean, inverse = statistics(total, square, images)
        values = [((v - mean) * inverse).reshape(deep, rows, lanes) for v in values]
        for c in range(nc):
            first, second = values[2 * c], values[2 * c + 1]
            even = jnp.where(keep, first, pltpu.roll(second, rows // 2, 1))
            odd = jnp.where(keep, pltpu.roll(first, rows // 2, 1), second)
            norm_ref[c * half : (c + 1) * half, span] = jnp.stack([even, odd], 1).reshape(half, lanes).astype(bf16)
        for k, term in enumerate(kernel_terms(mean, 3) + kernel_terms(inverse, 3)):
            tail[8 + k : 9 + k, span] = term
        tail[16:17, span] = inverse

    norm = norm_ref[...]
    copies = []
    for j in range(cols_a // cols):
        span = slice(j * cols, (j + 1) * cols)
        corr = dot(a_ref[:, span], norm, ((0,), (0,))) / images
        corr_ref[span, :] = corr
        place = pl.ds(j * cols, cols)
        copies.append(pltpu.make_async_copy(corr_ref.at[place], out_ref.at[place], sems.at[j]))
        copies[-1].start()
        tail[j : j + 1, :] = jnp.sum(corr * corr, 1)[None, :]
        high[span, :] = corr.astype(bf16)

    place = pl.multiple_of(idx[2] * cols, cols)
    corr = corr_ref[pl.ds(place, cols), :]
    row = lax.broadcasted_iota(jnp.int32, corr.shape, 0)
    col = lax.broadcasted_iota(jnp.int32, corr.shape, 1)
    diagonal = jnp.sum(jnp.where(row == col, corr, 0.0), 0, keepdims=True)
    for k, part in enumerate(kernel_terms(diagonal, 2)):
        tail[14 + k : 15 + k, :] = part
    shift = -2.0 * (1.0 - diagonal) - 2.0 * off_weight * diagonal
    shift = jnp.where(idx[3] == 1, shift, 0.0)
    chunk = images // nx
    totals = []
    for k in range(nx):
        span = slice(k * chunk, (k + 1) * chunk)
        total = dot(a_ref[span, :], high[...], ((1,), (0,))) * (2.0 * off_weight)
        totals.append(total + a_ref[span, pl.ds(place, cols)].astype(f32) * shift)
    along = 0.0
    for k in range(nx):
        along += jnp.sum(totals[k] * norm_ref[k * chunk : (k + 1) * chunk, :].astype(f32), 0, keepdims=True)
    along = along / images
    for k in range(nx):
        total = totals[k] - norm_ref[k * chunk : (k + 1) * chunk, :].astype(f32) * along
        to = k ^ idx[1]
        to = to ^ (to >> 1)
        part_ref[pl.ds(pl.multiple_of(to * chunk, chunk), chunk), :] = (total * tail[16:17, :]).astype(bf16)
    for copy in copies:
        copy.wait()


def tile(idx, norm_a, parts, sizes):
    nz, ny, nc, nx = sizes
    images, cols_a = norm_a.shape
    cols = parts.shape[2] * parts.shape[4]
    return pl.pallas_call(
        functools.partial(tile_kernel, nz, ny, nc, nx),
        out_shape=(
            jax.ShapeDtypeStruct((cols_a, cols), f32),
            jax.ShapeDtypeStruct((images, cols), bf16),
            jax.ShapeDtypeStruct((images, cols), bf16),
            jax.ShapeDtypeStruct((24, cols), f32),
        ),
        in_specs=[pl.BlockSpec(memory_space=pltpu.SMEM)] + in_vmem(2),
        out_specs=[pl.BlockSpec(memory_space=pl.ANY)] + in_vmem(3),
        scratch_shapes=[
            pltpu.VMEM((cols_a, cols), f32),
            pltpu.VMEM((cols_a, cols), bf16),
            pltpu.SemaphoreType.DMA((cols_a // cols,)),
        ],
        compiler_params=pltpu.CompilerParams(vmem_limit_bytes=VMEM_LIMIT),
        cost_estimate=pl.CostEstimate(
            flops=6 * images * cols_a * cols, bytes_accessed=4 * images * cols_a, transcendentals=0
        ),
    )(idx, norm_a, parts)


def gram_kernel(nz, ny, nc, nx, idx, norm_ref, tail, send_ref):
    images, cols = norm_ref.shape
    rows = images // (nz * ny * nc)
    take = rows // nx
    norm = norm_ref[...]
    picks = nz * ny * nc * take
    out = lax.broadcasted_iota(jnp.int32, (picks, images), 0)
    image = lax.broadcasted_iota(jnp.int32, (picks, images), 1)
    t, c, y, z = out & 1, (out >> 1) & 1, (out >> 2) & 3, out >> 4
    wanted = ((c * ny + y) * nz + z) * rows + idx[1] * take + t
    select = jnp.where(image == wanted, 1.0, 0.0).astype(bf16)
    picked = dot(select, norm, ((1,), (0,))).astype(bf16)
    gram = dot(picked, norm, ((1,), (1,)))
    for z in range(nz):
        send_ref[z, :, :images] = gram[z * 16 : z * 16 + 16].astype(bf16)

    values = tail[0:16, :].astype(bf16)
    for z in range(nz):
        send_ref[z, :, images:] = values


def gram_part(idx, norm_b, tail, sizes):
    nz = sizes[0]
    images, cols = norm_b.shape
    return pl.pallas_call(
        functools.partial(gram_kernel, *sizes),
        out_shape=jax.ShapeDtypeStruct((nz, 16, images + cols), bf16),
        in_specs=[pl.BlockSpec(memory_space=pltpu.SMEM)] + in_vmem(2),
        out_specs=in_vmem(1)[0],
        compiler_params=pltpu.CompilerParams(vmem_limit_bytes=VMEM_LIMIT),
        cost_estimate=pl.CostEstimate(
            flops=8 * images * images * cols, bytes_accessed=16 * images * cols, transcendentals=0
        ),
    )(idx, norm_b, tail)


def finish_kernel(nz, ny, nc, got_ref, norm_ref, shifted_ref, scale_ref, grad_a_ref, grad_b_ref, gram):
    nx, rows_x, cols = got_ref.shape
    images = norm_ref.shape[0]
    rows = shifted_ref.shape[0]
    n_rows = images // nx
    wide = images // cols
    take = rows // nx
    for x in range(nx):
        values = got_ref[x, n_rows:, :].astype(f32)
        for part in range(2):
            for t in range(take):
                for w in range(wide):
                    line = (part * take + t) * wide + w
                    to = part * rows + x * take + t
                    gram[to : to + 1, w * cols : (w + 1) * cols] = values[line : line + 1]
    both = dot(gram[...].astype(bf16), norm_ref[...], ((1,), (0,)))
    grad_a_ref[...] = (both[:rows] + both[rows:]) * scale_ref[...] + shifted_ref[...]
    for x in range(nx):
        values = got_ref[x, :n_rows, :].astype(f32)
        for k in range(n_rows // rows):
            block = x * (n_rows // rows) + k
            c, y, z = block // (ny * nz), block // nz % ny, block % nz
            to = ((z * ny + y) * nc + c) * rows
            grad_b_ref[to : to + rows, :] = values[k * rows : (k + 1) * rows]


def finish(got, norm_a, shifted, scale, sizes):
    images, cols_a = norm_a.shape
    rows, cols = shifted.shape[0], got.shape[2]
    return pl.pallas_call(
        functools.partial(finish_kernel, *sizes[:3]),
        out_shape=(
            jax.ShapeDtypeStruct((rows, cols_a), f32),
            jax.ShapeDtypeStruct((images, cols), f32),
        ),
        in_specs=in_vmem(4),
        out_specs=in_vmem(2),
        scratch_shapes=[pltpu.VMEM((2 * rows, images), f32)],
        compiler_params=pltpu.CompilerParams(vmem_limit_bytes=VMEM_LIMIT),
    )(got, norm_a, shifted, scale)


def local(view_a, view_b):
    nz, ny, nc = (lax.axis_size(a) for a in DP)
    nh, nx = (lax.axis_size(a) for a in FEAT)
    rows, cols_a = view_a.shape
    width = view_b.shape[1]
    cols_b = width // (nz * ny * nc)
    images = rows * nz * ny * nc
    iz, iy, ic = (lax.axis_index(a) for a in DP)
    ih, ix = (lax.axis_index(a) for a in FEAT)
    feat = ih * nx + ix
    n_yc = ny * nc

    with jax.named_scope("gather_z"):
        lanes = cols_b // 2
        idx = jnp.stack([ic, ix, iy * nc + ic, (feat == iz).astype(jnp.int32)]).astype(jnp.int32)
        quarter = view_b.reshape(2, rows // 2, nz * ny, nc, 2, lanes)
        quarter = lax.dynamic_index_in_dim(quarter, ix // 2, 0, False)
        quarter = lax.dynamic_index_in_dim(quarter, ix % 2, 3, False)
        quarter = quarter.transpose(2, 0, 1, 3).reshape(rows, nz, ny * lanes).transpose(1, 0, 2)
        send = jnp.concatenate([jnp.broadcast_to(view_a[None], (nz, rows, cols_a)), quarter], 2)
        got = exchange(send, "zl").reshape(nz * rows, cols_a + ny * lanes)
    with jax.named_scope("gather_y"):
        send = jnp.concatenate(
            [
                jnp.broadcast_to(got[None, :, :cols_a], (ny, nz * rows, cols_a)),
                got[:, cols_a:].reshape(nz * rows, ny, lanes).transpose(1, 0, 2),
            ],
            2,
        )
        got = exchange(send, "y").reshape(ny * nz * rows, cols_a + lanes)
    with jax.named_scope("gather_core_x"):
        got_other = lax.ppermute(got, "c", SWAP)
        half = images // nc
        parts = got[:, cols_a:].reshape(half // rows, nc, rows // nc, lanes).transpose(1, 0, 2, 3)
        parts = parts.reshape(nc, 1, half // nc, lanes)
        parts = jnp.broadcast_to(parts, (nc, nx, half // nc, lanes)).reshape(nc * nx, half // nc, lanes)
        parts = exchange(parts, ("c", "x")).reshape(nc, nx // 2, 2, half // nc, lanes)
    with jax.named_scope("standardize_a"):
        norm_a, stat_a = standardize_a(idx, got, got_other, cols_a)
        norm_a, parts = lax.optimization_barrier((norm_a, parts))
        mean_a, inverse_a = stat_a[0], stat_a[1]
    with jax.named_scope("tile"):
        correlation, part_b, norm_b, tail = tile(idx, norm_a, parts, (nz, ny, nc, nx))

    with jax.named_scope("sum_b_x_reduce_z"):
        n_rows = images // nx
        came = lax.ppermute(part_b[2 * n_rows :], "x", [(i, i ^ 3) for i in range(nx)])
        send = gram_part(idx, norm_b, tail, (nz, ny, nc, nx))
        got = exchange(send, "zl")
        sum_b = part_b[: 2 * n_rows].astype(f32) + came.astype(f32)
        came = lax.ppermute(sum_b[n_rows:].astype(bf16), "x", [(i, i ^ 1) for i in range(nx)])
        sum_b = (sum_b[:n_rows] + came.astype(f32)).astype(bf16)
    with jax.named_scope("reduce_yc"):
        take = rows // nx
        total = jnp.sum(got[:, :, :images].astype(f32), 0).reshape(n_yc, take * images // cols_b, cols_b)
        squares = jnp.sum(got[:, :8, images:].astype(f32), 0)
        aux = lax.dynamic_index_in_dim(got[:, 8:, images:], feat, 0, False).astype(f32)
        aux = jnp.stack([aux[0] + aux[1] + aux[2], aux[3] + aux[4] + aux[5], aux[6] + aux[7], aux[7]])
        right = jnp.concatenate([total, jnp.broadcast_to(aux[None], (n_yc, 4, cols_b))], 1)
        left = jnp.broadcast_to(squares[None], (n_yc, 8, cols_b))
        send = jnp.concatenate([left, right, jnp.zeros((n_yc, 8, 2 * cols_b), f32)], 2)
        other = lax.ppermute(sum_b, "zh", SWAP)
        got = exchange(send, ("y", "c"))[:, :, : 2 * cols_b]
        squares = jnp.sum(got[:, :, :cols_b], 0).reshape(cols_a)
        gram = jnp.sum(got[:, :4, cols_b:], 0)
        mean_f, inverse_f, diag_f = (got[:, 4 + k, cols_b:].reshape(cols_a) for k in range(3))

    with jax.named_scope("shift_a"):
        shift = -2.0 * (1.0 - diag_f) - 2.0 * off_weight * diag_f
        projected = 2.0 * off_weight * squares + shift * diag_f
        own_b = ((view_b_columns(view_b, feat, cols_a) - mean_f) * inverse_f).astype(bf16).astype(f32)
        own_a = ((view_a.astype(f32) - mean_a) * inverse_a).astype(bf16).astype(f32)
        shifted = (own_b * shift - own_a * projected) * inverse_a
        scale = jnp.broadcast_to(2.0 * off_weight / images * inverse_a, (rows, cols_a))
    with jax.named_scope("gather_b_x"):
        sum_b = (sum_b.astype(f32) + other.astype(f32)).astype(bf16)
        upper, lower = terms(gram, 2)
        own = jnp.concatenate([sum_b, upper, lower, jnp.zeros((8, cols_b), bf16)], 0)
        shifted, scale = lax.optimization_barrier((shifted, scale))
        got = exchange(jnp.broadcast_to(own[None], (nx,) + own.shape), "x")
    with jax.named_scope("finish"):
        grad_a, grad_b = finish(got, norm_a, shifted, scale, (nz, ny, nc, nx))
    return correlation, grad_a, grad_b


def view_b_columns(view_b, feat, cols_a):
    return lax.dynamic_slice_in_dim(view_b, feat * cols_a, cols_a, 1).astype(f32)


def solution(mesh):
    sizes = (8, 4, 2, 2, 4)
    fine = Mesh(mesh.devices.reshape(sizes), AXES)
    in_specs = (P(DP, FEAT), P(DP, None))
    out_specs = (P(FEAT, DP), P(DP, FEAT), P(None, DP))
    return jax.shard_map(local, mesh=fine, in_specs=in_specs, out_specs=out_specs, check_vma=False)
```
